512 devices in a mesh: row: 16 (over z_hi, x, core), col: 32 (over z_lo, y).
Axes of the slice: x: 4, y: 4, z: 16 (z_hi: 2, z_lo: 8; z = z_hi * 8 + z_lo), core: 2. Of those that a mesh axis runs over, the one named last changes fastest.
Arguments:
- noisy_image: bfloat16 [512, 256, 256], P('row', 'col'), may hold values from -6 to 6
- time_index: int32 [1], replicated, may hold values from 0 to 31
- solver_index: int32 [1], replicated, may hold values from 0 to 31
- time_gains: float32 [32, 256], replicated, may hold values from 0.5 to 1.5
- pixel_qkv: bfloat16 [256, 768], replicated, may hold values from -0.375 to 0.375
- pixel_out: bfloat16 [256, 256], replicated, may hold values from -0.375 to 0.375
- coarse_gains: float32 [32, 1024], replicated, may hold values from 0.5 to 1.5
- coarse_qkv: bfloat16 [1024, 16, 192], P(None, 'row'), may hold values from -0.1875 to 0.1875
- coarse_out: bfloat16 [1024, 1024], P('row'), may hold values from -1.5 to 1.5
- upsample_weight: bfloat16 [1024, 1024], replicated, may hold values from -0.1875 to 0.1875
- skip_gain: float32 [256], replicated, may hold values from 0.5 to 1.5
- solver_table: float32 [32, 2], replicated, may hold values from 0.3 to 1
Outputs:
- next_image: float32 [512, 256, 256], P('row', 'col')
The draws below stay inside these ranges and needn't reach their ends.
All inputs are finite; a program needn't handle non-finite values.
Results may differ from the reference program's by a relative error of at most 0.02.
Values may be sent and summed in bfloat16 or wider, within the bound.
A program may use at most 64 MiB of HBM per device.

```python
import math
import jax
import jax.numpy as jnp
from jax import lax

WIDTH = 256
HEAD_DIM = 64
WINDOW = 7
STEPS = 32
TILE_COLS = 8
COARSE_WIDTH = 1024
PIX_HEADS = 4
HEADS = 16
IMG_ROWS = 512
IMG_COLS = 256
N_ROW = 16
N_COL = 32


def block_levels(rng, extent, split, smallest, largest):
    factor_of, own = 1.0, jax.random.fold_in(rng, 6)
    for position, parts in split:
        steps = jnp.exp(jax.random.uniform(jax.random.fold_in(own, position), (parts,), jnp.float32, smallest / len(split), largest / len(split)))
        factor_of = factor_of * jnp.repeat(steps, extent[position] // parts).reshape([-1 if axis == position else 1 for axis in range(len(extent))])
    return factor_of


def centred(rng, shape, scale, most, split=(), held_as=jnp.bfloat16):
    factor_of = block_levels(rng, shape, split, -0.22, 0.18) if split else 1.0
    drawn = jax.random.normal(rng, shape, jnp.float32) * scale * factor_of
    return jnp.minimum(jnp.maximum(drawn, -most), most).astype(held_as)


def setup_inputs(seed: int = 0) -> dict:
    splits = jax.random.split(jax.random.key(seed), 13)
    noisy_image = centred(splits[0], (IMG_ROWS, IMG_COLS, WIDTH), 1.0, 6.0, ((0, 16), (1, 32)))
    time_index = jax.random.randint(splits[1], (1,), 0, STEPS).astype(jnp.int32)
    solver_index = jax.random.randint(splits[2], (1,), 0, STEPS).astype(jnp.int32)
    time_gains = jnp.clip(jax.random.uniform(splits[3], (STEPS, WIDTH), jnp.float32, 0.5, 1.5), 0.5, 1.5)
    pixel_qkv = centred(splits[4], (WIDTH, 3 * WIDTH), WIDTH ** -0.5, 0.375)
    pixel_out = centred(splits[5], (WIDTH, WIDTH), WIDTH ** -0.5, 0.375)
    coarse_gains = jnp.clip(jax.random.uniform(splits[6], (STEPS, COARSE_WIDTH), jnp.float32, 0.5, 1.5), 0.5, 1.5)
    coarse_qkv = centred(splits[7], (COARSE_WIDTH, HEADS, 3 * HEAD_DIM), COARSE_WIDTH ** -0.5, 0.1875, ((1, 16),))
    coarse_out = centred(splits[8], (COARSE_WIDTH, COARSE_WIDTH), (COARSE_WIDTH // 64) ** -0.5, 1.5, ((0, 16),))
    upsample_weight = centred(splits[9], (COARSE_WIDTH, 4 * WIDTH), COARSE_WIDTH ** -0.5, 0.1875)
    skip_gain = jnp.clip(jax.random.uniform(splits[10], (WIDTH,), jnp.float32, 0.5, 1.5), 0.5, 1.5)
    solver_table = jnp.clip(jax.random.uniform(splits[11], (STEPS, 2), jnp.float32, 0.3, 1.0), 0.3, 1.0)
    return {"noisy_image": noisy_image, "time_index": time_index, "solver_index": solver_index, "time_gains": time_gains, "pixel_qkv": pixel_qkv, "pixel_out": pixel_out, "coarse_gains": coarse_gains, "coarse_qkv": coarse_qkv, "coarse_out": coarse_out, "upsample_weight": upsample_weight, "skip_gain": skip_gain, "solver_table": solver_table}


def root_norm(values, scales):
    floats = values.astype(jnp.float32)
    factor = lax.rsqrt(lax.optimization_barrier(jnp.mean(floats * floats, -1, keepdims=True)) + 1e-06)
    return (floats * factor * scales).astype(jnp.bfloat16)

def window_attention(query, keys, values, inside):
    rows, cols = (query.shape[0], query.shape[1])
    query_f = query.astype(jnp.float32)
    score_list = []
    for shift_row in range(WINDOW):
        for shift_col in range(WINDOW):
            keyed = keys[shift_row:shift_row + rows, shift_col:shift_col + cols].astype(jnp.float32)
            scored = lax.optimization_barrier(jnp.sum(query_f * keyed, -1)) / math.sqrt(HEAD_DIM)
            usable = inside[shift_row:shift_row + rows, shift_col:shift_col + cols][:, :, None]
            score_list.append(jnp.where(usable, scored, -1e+30))
    weights = jax.nn.softmax(jnp.stack(score_list, -1), -1).astype(jnp.bfloat16)
    total = jnp.zeros(query.shape, jnp.float32)
    for shift_row in range(WINDOW):
        for shift_col in range(WINDOW):
            offset = shift_row * WINDOW + shift_col
            valued = values[shift_row:shift_row + rows, shift_col:shift_col + cols].astype(jnp.float32)
            total = total + weights[..., offset, None].astype(jnp.float32) * valued
    return total.astype(jnp.bfloat16)

def reference(noisy_image, time_index, solver_index, time_gains, pixel_qkv, pixel_out, coarse_gains, coarse_qkv, coarse_out, upsample_weight, skip_gain, solver_table):
    reach = WINDOW // 2
    normed = root_norm(noisy_image, time_gains[time_index[0]])
    projected = jnp.dot(normed.reshape(-1, WIDTH), pixel_qkv, preferred_element_type=jnp.float32)
    projected = projected.astype(jnp.bfloat16).reshape(IMG_ROWS, IMG_COLS, 3, PIX_HEADS, HEAD_DIM)
    padding = ((reach, reach), (reach, reach), (0, 0), (0, 0))
    inside = jnp.pad(jnp.ones((IMG_ROWS, IMG_COLS), jnp.bool_), reach)
    attended = window_attention(projected[:, :, 0], jnp.pad(projected[:, :, 1], padding), jnp.pad(projected[:, :, 2], padding), inside)
    mixed = jnp.dot(attended.reshape(-1, WIDTH), pixel_out, preferred_element_type=jnp.float32)
    pixels = (noisy_image.astype(jnp.float32) + mixed.reshape(IMG_ROWS, IMG_COLS, WIDTH)).astype(jnp.bfloat16)
    half_rows, half_cols, strip_cols = (IMG_ROWS // 2, IMG_COLS // 2, TILE_COLS // 2)
    merged = pixels.reshape(half_rows, 2, half_cols, 2, WIDTH).transpose(0, 2, 1, 3, 4)
    merged = merged.reshape(half_rows, half_cols, COARSE_WIDTH)
    merged_normed = root_norm(merged, coarse_gains[time_index[0]])
    strips = merged_normed.reshape(half_rows, N_COL, strip_cols, COARSE_WIDTH).transpose(1, 0, 2, 3)
    strips = strips.reshape(N_COL, half_rows * strip_cols, COARSE_WIDTH)
    group_width = COARSE_WIDTH // N_ROW
    grouped_weight = coarse_out.reshape(N_ROW, group_width, COARSE_WIDTH).astype(jnp.float32)

    def strip_attention(tokens):
        count = tokens.shape[0]
        proj = jnp.einsum('nc,chk->nhk', tokens.astype(jnp.float32), coarse_qkv.astype(jnp.float32))
        proj = proj.astype(jnp.bfloat16).astype(jnp.float32)
        query = proj[..., :HEAD_DIM]
        keyed = proj[..., HEAD_DIM:2 * HEAD_DIM]
        valued = proj[..., 2 * HEAD_DIM:]
        scores = jnp.einsum('qhd,khd->hqk', query, keyed) / math.sqrt(HEAD_DIM)
        weights = jax.nn.softmax(scores, -1).astype(jnp.bfloat16).astype(jnp.float32)
        outputs = jnp.einsum('hqk,khd->qhd', weights, valued).astype(jnp.bfloat16)
        grouped = outputs.reshape(count, N_ROW, group_width).astype(jnp.float32)
        partial_sums = jnp.einsum('ngk,gkd->gnd', grouped, grouped_weight).astype(jnp.bfloat16)
        partial_sums = lax.optimization_barrier(partial_sums)
        return lax.optimization_barrier(jnp.sum(partial_sums.astype(jnp.float32), 0))
    delta = lax.map(strip_attention, strips)
    delta = delta.reshape(N_COL, half_rows, strip_cols, COARSE_WIDTH).transpose(1, 0, 2, 3)
    delta = delta.reshape(half_rows, half_cols, COARSE_WIDTH)
    coarse_next = (merged.astype(jnp.float32) + delta).astype(jnp.bfloat16)
    upsampled = jnp.dot(coarse_next.reshape(-1, COARSE_WIDTH), upsample_weight, preferred_element_type=jnp.float32)
    upsampled = upsampled.reshape(half_rows, half_cols, 2, 2, WIDTH).transpose(0, 2, 1, 3, 4)
    upsampled = upsampled.reshape(IMG_ROWS, IMG_COLS, WIDTH)
    denoised = upsampled + skip_gain * pixels.astype(jnp.float32)
    coefficients = solver_table[solver_index[0]]
    return coefficients[0] * noisy_image.astype(jnp.float32) + coefficients[1] * denoised
```

```python
import jax
import jax.numpy as jnp
from jax import lax
from jax.experimental import pallas as pl
from jax.experimental.pallas import tpu as pltpu
from jax.sharding import PartitionSpec as P

MESH = pl.DeviceIdType.MESH
BF = jnp.bfloat16
F32 = jnp.float32
ROWS, COLS = 16, 32
TOKENS = 64
WIDE = 1024
CHUNKS = 4
PER = TOKENS // CHUNKS
DIRS = ((-1, 0), (1, 0), (0, -1), (0, 1), (-1, -1), (-1, 1), (1, -1), (1, 1))


def iota(shape, dim):
    return lax.broadcasted_iota(jnp.int32, shape, dim)


def nt(left, right):
    return lax.dot_general(left, right, (((1,), (1,)), ((), ())), preferred_element_type=F32)


def mm(left, right):
    return jnp.dot(left, right, preferred_element_type=F32)


def norm(floats, scales):
    factor = lax.rsqrt(jnp.mean(floats * floats, -1, keepdims=True) + 1e-06)
    return (floats * factor * scales).astype(BF)


def pick(table, index):
    hit = iota(table.shape, 0) == index
    return jnp.sum(jnp.where(hit, table, 0.0), 0, keepdims=True)


def kernel(
    time_ref,
    step_ref,
    noisy_hbm,
    solver_hbm,
    gains_hbm,
    qkv_hbm,
    pout_hbm,
    cgains_hbm,
    skip_hbm,
    cqkv_hbm,
    cout_hbm,
    up_hbm,
    out_ref,
    noisy_ref,
    solver_ref,
    gains_ref,
    qkv_ref,
    pout_ref,
    cgains_ref,
    skip_ref,
    cc,
    ll,
    rr,
    pack_l,
    pack_r,
    kv_c,
    kv_e,
    query,
    noisy_m,
    merged,
    own,
    tok,
    wt,
    w3,
    wo,
    wup,
    asked_all,
    keys_all,
    values_all,
    ret_s,
    ret_r,
    halo_s,
    halo_r,
    z_s,
    z_r,
    xr_s,
    xr_r,
    xl_s,
    xl_r,
    xf_s,
    xf_r,
    sib_s,
    sib_r,
    w1_s,
    w1_r,
    wx_s,
    wx_r,
    w2_s,
    w2_r,
    w3_s,
    w3_r,
    w4_s,
    w4_r,
    back_s,
    back_r,
    local,
):
    row, col = lax.axis_index("row"), lax.axis_index("col")
    half, xx, core = row // 8, (row // 2) % 4, row % 2
    yy = col % 4
    group = row // 2
    far_col = jnp.where(col >= 16, col - 16, col + 16)
    far_row = jnp.where(row >= 8, row - 8, row + 8)
    sibling = row + 1 - 2 * core

    fourth = jnp.where(row == 8, 0, 3)
    third = 3 - fourth

    def x_row(shift):
        return half * 8 + ((xx + shift) % 4) * 2 + core

    def y_col(shift):
        return col - yy + (yy + shift) % 4

    def remote(src, dst, send, recv, where):
        return pltpu.make_async_remote_copy(
            src_ref=src, dst_ref=dst, send_sem=send, recv_sem=recv, device_id=where, device_id_type=MESH
        )

    def arrive(dst, recv, send):
        remote(dst, dst, send, recv, (row, col)).wait_recv()

    sent = []

    def send(*args):
        remote(*args).start()

    def sent_by(sem, ref):
        sent.append((sem, ref))

    def wait_sent():
        for sem, ref in sent:
            remote(ref, ref, sem, local.at[0], (row, col)).wait_send()
        sent.clear()

    def load(src, dst, at):
        copy = pltpu.make_async_copy(src, dst, local.at[at])
        copy.start()
        return copy

    load_noisy = load(noisy_hbm, noisy_ref, 3)

    barrier = pltpu.get_barrier_semaphore()

    def greet(where):
        pl.semaphore_signal(barrier, inc=1, device_id=where, device_id_type=MESH)

    there = []
    for down, right in DIRS:
        r, c = row + down, col + right
        there.append((r >= 0) & (r < ROWS) & (c >= 0) & (c < COLS))
    for d, (down, right) in enumerate(DIRS):

        @pl.when(there[d])
        def _():
            greet((row + down, col + right))

    greet((row, far_col))
    greet((far_row, far_col))
    for shift in (1, 2, 3):
        greet((x_row(shift), col))
        greet((row, y_col(shift)))
    greet((sibling, col))
    partners = 2 + 6 + 1
    for flag in there:
        partners = partners + flag.astype(jnp.int32)

    quarter = pl.ds(pl.multiple_of(yy * 16, 16), 16)
    own_quarter = wo.at[group, core, quarter]
    quarter = pl.ds(pl.multiple_of(yy * 16, 16), 16)
    own_quarter = wo.at[group, core, quarter]
    own_block = wo.at[group, core]
    load_wo = load(cout_hbm, own_block, 0)
    load_gains = load(gains_hbm, gains_ref, 4)
    load_qkv = load(qkv_hbm, qkv_ref, 5)
    load_pout = load(pout_hbm, pout_ref, 6)
    load_cgains = load(cgains_hbm, cgains_ref, 7)
    load_wt = load(cqkv_hbm, wt, 1)
    load_skip = load(skip_hbm, skip_ref, 8)
    load_solver = load(solver_hbm, solver_ref, 9)
    load_up = load(up_hbm, wup, 2)

    load_noisy.wait()
    tile = noisy_ref[...].astype(F32).reshape(256, 256)
    tile_b = tile.astype(BF)
    cc[32:288, :] = tile_b
    spot = iota((128, 256), 0)
    place = (spot >> 2) * 8 + (spot & 3)
    lane = iota((128, 256), 1)
    pack_l[...] = mm((lane == place).astype(F32).astype(BF), tile_b).astype(BF)
    pack_r[...] = mm((lane == place + 4).astype(F32).astype(BF), tile_b).astype(BF)

    pl.semaphore_wait(barrier, partners)

    halo = (
        (cc.at[32:64], cc.at[288:320]),
        (cc.at[256:288], cc.at[0:32]),
        (pack_l, rr.at[16:144]),
        (pack_r, ll.at[16:144]),
        (pack_l.at[0:16], rr.at[144:160]),
        (pack_r.at[0:16], ll.at[144:160]),
        (pack_l.at[112:128], rr.at[0:16]),
        (pack_r.at[112:128], ll.at[0:16]),
    )

    def halo_copy(d):
        src, dst = halo[d]
        return remote(src, dst, halo_s.at[d], halo_r.at[d], (row + DIRS[d][0], col + DIRS[d][1]))

    for d in (2, 3, 0, 1, 4, 5, 6, 7):

        @pl.when(there[d])
        def _():
            halo_copy(d).start()

    from_there = []
    for down, right in DIRS:
        r, c = row - down, col - right
        from_there.append((r >= 0) & (r < ROWS) & (c >= 0) & (c < COLS))
    for d in range(8):

        @pl.when(jnp.logical_not(from_there[d]))
        def _():
            dst = halo[d][1]
            dst[...] = jnp.zeros(dst.shape, BF)

    load_wo.wait()
    send(own_quarter, own_quarter, w1_s.at[0], w1_r.at[0], (far_row, far_col))
    sent_by(w1_s.at[0], own_quarter)
    for shift in (1, 2, 3):
        send(own_block, own_block, wx_s.at[0], wx_r.at[0], (x_row(shift), col))
    three = pl.ds(0, 3)
    sent_by(wx_s.at[0], wo.at[three, core])

    load_gains.wait()
    scales = pick(gains_ref[...], time_ref[0])
    normed = norm(tile, scales)
    load_qkv.wait()
    kv_c[32:288, :] = mm(normed, qkv_ref[:, 256:768]).astype(BF)
    i = iota((256, 256), 0)
    spot, a, b, p, q = i >> 6, (i >> 5) & 1, (i >> 4) & 1, (i >> 2) & 3, i & 3
    blk = jnp.where(spot < 2, spot + 1, jnp.where(spot == 2, third, fourth))
    source = (8 * blk + 2 * p + a) * 8 + 2 * q + b
    shuffle = (iota((256, 256), 1) == source).astype(F32).astype(BF)
    noisy_q = mm(shuffle, tile_b)
    normed_q = mm(shuffle, normed).astype(BF)
    query[...] = mm(normed_q, qkv_ref[:, 0:256]).astype(BF)
    noisy_qb = noisy_q.astype(BF)
    for block in range(4):
        for ab in range(4):
            at = block * 64 + ab * 16
            noisy_m[block * 16 : block * 16 + 16, ab * 256 : ab * 256 + 256] = noisy_qb[at : at + 16]

    load_wt.wait()
    w3[0:64, :] = (wt[0:64, :].astype(F32) * 0.125).astype(BF)
    w3[64:192, :] = wt[64:192, :]
    w3[192:256, :] = jnp.zeros((64, WIDE), BF)

    def halo_wait(d, flag):
        @pl.when(from_there[d] & flag)
        def _():
            arrive(halo[d][1], halo_r.at[d], halo_s.at[d])

    def edge_kv(array):
        return mm(norm(array.astype(F32), scales), qkv_ref[:, 256:768]).astype(BF)

    halo_wait(2, True)
    halo_wait(3, True)
    sides = edge_kv(jnp.concatenate([ll[16:144, :], rr[16:144, :]], 0))
    kv_e[16:144, :] = sides[0:128]
    kv_e[176:304, :] = sides[128:256]

    def outer_edge(block, last):
        above = (row == 8) if last else (row != 8)
        for d in (1, 6, 7):
            halo_wait(d, above)
        for d in (0, 4, 5):
            halo_wait(d, jnp.logical_not(above))
        wide = pl.ds(pl.multiple_of(jnp.where(block == 0, 0, 288), 32), 32)
        start = jnp.where(block == 0, 0, 144)
        narrow = pl.ds(pl.multiple_of(start, 16), 16)
        result = edge_kv(jnp.concatenate([cc[wide, :], ll[narrow, :], rr[narrow, :]], 0))
        kv_c[wide, :] = result[0:32]
        kv_e[narrow, :] = result[32:48]
        kv_e[pl.ds(pl.multiple_of(160 + start, 16), 16), :] = result[48:64]

    j = iota((64, 256), 1)
    in_c = j < 128
    key_row = jnp.where(in_c, j >> 3, (j & 63) >> 2) - 4
    key_col = jnp.where(in_c, j & 7, (j & 3) + jnp.where(j < 192, -4, 8))
    i = iota((64, 256), 0)
    query_row = 2 * ((i >> 2) & 3) + ((i >> 5) & 1)
    query_col = 2 * (i & 3) + ((i >> 4) & 1)
    full_col = key_col + col * 8
    near = (
        (jnp.abs(key_row - query_row) <= 3)
        & (jnp.abs(key_col - query_col) <= 3)
        & (full_col >= 0)
        & (full_col < 256)
    )
    head_of = iota((64, 256), 1) >> 6
    ones = jnp.ones((256, 256), BF)
    load_cgains.wait()
    load_pout.wait()
    coarse_scales = pick(cgains_ref[...], time_ref[0])

    def window_block(spot, block):
        inner = pl.ds(pl.multiple_of(64 * block, 64), 128)
        lefts = pl.ds(pl.multiple_of(32 * block, 32), 64)
        rights = pl.ds(pl.multiple_of(160 + 32 * block, 32), 64)
        keys = jnp.concatenate([kv_c[inner, 0:256], kv_e[lefts, 0:256], kv_e[rights, 0:256]], 0)
        values = jnp.concatenate([kv_c[inner, 256:512], kv_e[lefts, 256:512], kv_e[rights, 256:512]], 0)
        asked = query[64 * spot : 64 * spot + 64, :].astype(F32) * 0.125
        spread = jnp.concatenate([jnp.where(head_of == h, asked, 0.0) for h in range(4)], 0).astype(BF)
        full_row = key_row + (row * 32 + 8 * block)
        usable = near & (full_row >= 0) & (full_row < 512)
        bias = jnp.where(usable, 0.0, -1e30)
        scores = nt(spread, keys) + jnp.concatenate([bias] * 4, 0)
        weights = jnp.exp(scores - jnp.max(scores, 1, keepdims=True)).astype(BF)
        sums = mm(weights, ones)
        mixed = mm(weights, values)
        total, share = jnp.zeros((64, 256), F32), jnp.zeros((64, 256), F32)
        for h in range(4):
            total = jnp.where(head_of == h, sums[64 * h : 64 * h + 64], total)
            share = jnp.where(head_of == h, mixed[64 * h : 64 * h + 64], share)
        attended = (share / total).astype(BF)
        delta = mm(attended, pout_ref[...])
        for ab in range(4):
            rows, lanes = pl.ds(spot * 16, 16), pl.ds(ab * 256, 256)
            pixels = noisy_m[rows, lanes].astype(F32) + delta[ab * 16 : ab * 16 + 16]
            merged[rows, lanes] = pixels.astype(BF)

    def part(k):
        return pl.ds(k * PER, PER)

    for k in range(CHUNKS):
        if k < 2:
            window_block(k, k + 1)
        else:
            outer_edge(third if k == 2 else fourth, k == 3)
            window_block(k, third if k == 2 else fourth)
        own[part(k), :] = norm(merged[part(k), :].astype(F32), coarse_scales)
        for t, target in enumerate((row, far_row)):
            send(
                own.at[part(k)],
                tok.at[half, xx, core, part(k)],
                z_s.at[t],
                z_r.at[k],
                (target, far_col),
            )
    for t in range(2):
        sent_by(z_s.at[t], own)

    near_blocks = pl.ds(pl.multiple_of(half * 4, 4), 4)
    far_blocks = pl.ds(pl.multiple_of(4 - half * 4, 4), 4)

    def weights_x():
        ref = wo.at[far_row // 2, core, quarter]
        arrive(ref, w1_r.at[0], w1_s.at[0])
        for shift in (1, 2, 3):
            send(ref, ref, w2_s.at[0], w2_r.at[0], (x_row(shift), col))
        sent_by(w2_s.at[0], wo.at[three, core, quarter])

    def weights_y():
        arrive(wo.at[three, core, quarter], w2_r.at[0], w2_s.at[0])
        ref = wo.at[far_blocks, core, quarter]
        for shift in (1, 2, 3):
            send(ref, ref, w3_s.at[0], w3_r.at[0], (row, y_col(shift)))
        sent_by(w3_s.at[0], wo.at[far_blocks, core, pl.ds(0, 48)])

    def weights_near():
        arrive(wo.at[three, core], wx_r.at[0], wx_s.at[0])
        ref = wo.at[near_blocks, core]
        send(ref, ref, w4_s.at[0], w4_r.at[0], (sibling, col))
        sent_by(w4_s.at[0], ref)

    def weights_far():
        arrive(wo.at[far_blocks, core, pl.ds(0, 48)], w3_r.at[0], w3_s.at[0])
        ref = wo.at[far_blocks, core]
        send(ref, ref, w4_s.at[1], w4_r.at[1], (sibling, col))
        sent_by(w4_s.at[1], ref)

    def blocks(shift, k, which=core):
        return tok.at[:, (xx + shift) % 4, which, part(k)]

    def one(side, shift, k):
        return tok.at[side, (xx + shift) % 4, core, part(k)]

    def to_sibling(shift, k):
        ref = blocks(shift, k)
        send(ref, ref, sib_s.at[0], sib_r.at[k], (sibling, col))

    def gather(k):
        ref = blocks(0, k)
        arrive(ref, z_r.at[k], z_s.at[0])
        send(ref, ref, xr_s.at[0], xr_r.at[k], (x_row(1), col))
        send(ref, ref, xl_s.at[0], xl_r.at[k], (x_row(3), col))
        to_sibling(0, k)

    def relay(k):
        arrive(blocks(3, k), xr_r.at[k], xr_s.at[0])
        ref = one(0, 3, k)
        send(ref, ref, xf_s.at[0], xf_r.at[k], (x_row(1), col))
        to_sibling(3, k)
        arrive(blocks(1, k), xl_r.at[k], xl_s.at[0])
        ref = one(1, 1, k)
        send(ref, ref, xf_s.at[1], xf_r.at[k], (x_row(3), col))
        to_sibling(1, k)

    def finish(k):
        arrive(blocks(2, k), xf_r.at[k], xf_s.at[0])
        to_sibling(2, k)

    def from_sibling(k):
        arrive(tok.at[:, :, 1 - core, part(k)], sib_r.at[k], sib_s.at[0])

    left = iota((16 * PER, 128), 1) < 64

    def project(k):
        tokens = tok[:, :, :, k * PER : (k + 1) * PER, :].reshape(16 * PER, WIDE)
        result = nt(tokens, w3[...])
        both, value = result[:, 0:128], result[:, 128:256]
        for ref, array in (
            (asked_all, jnp.where(left, both, 0.0)),
            (keys_all, pltpu.roll(both, 64, 1)),
            (values_all, jnp.where(left, value, 1.0)),
        ):
            ref[:, :, :, k * PER : (k + 1) * PER, :] = array.astype(BF).reshape(2, 4, 2, PER, 128)

    weights_x()
    gather(0)
    weights_y()
    relay(0)
    for k in range(1, CHUNKS):
        gather(k)
        finish(k - 1)
        relay(k)
        if k == 2:
            weights_near()
        from_sibling(k - 1)
        project(k - 1)
    finish(CHUNKS - 1)
    from_sibling(CHUNKS - 1)
    project(CHUNKS - 1)

    low = iota((32, 128), 1) < 64
    keys = keys_all[...].reshape(WIDE, 128)
    values = values_all[...].reshape(WIDE, 128)

    turns = (2, 1, 3, 0)

    def score(turn):
        return nt(asked_all[:, (xx + turns[turn]) % 4].reshape(256, 128), keys)

    whole = tok.at[:, xx, core]
    for sem in (xr_s.at[0], xl_s.at[0]):
        sent_by(sem, whole)
    for side in range(2):
        sent_by(xf_s.at[side], tok.at[side, xx, core])
    sent_by(sib_s.at[0], tok.at[:, :, core])

    scores = score(0)
    for turn in range(4):
        following = score(turn + 1) if turn < 3 else None
        weights = jnp.exp(scores - jnp.max(scores, 1, keepdims=True)).astype(BF)
        mixed = mm(weights, values)
        mixed = mixed / pltpu.roll(mixed, 64, 1)
        for which in range(4):
            at = 64 * which
            packed = jnp.where(low, mixed[at : at + 32], pltpu.roll(mixed[at + 32 : at + 64], 64, 1))
            ret_s[turn, which] = packed.astype(BF)
        for which in range(4):
            target = (which // 2) * 8 + ((xx + turns[turn]) % 4) * 2 + which % 2
            send(
                ret_s.at[turn, which],
                ret_r.at[turn, 2 * half + core],
                back_s.at[0],
                back_r.at[turn],
                (target, far_col),
            )
        scores = following

    weights_far()

    load_up.wait()
    load_skip.wait()
    load_solver.wait()
    pixels = merged[...].astype(F32)
    table = solver_ref[...]
    table = jnp.where(iota(table.shape, 1) == step_ref[0], table, 0.0)
    keep = jnp.sum(table[0:1], 1, keepdims=True)
    gain = jnp.sum(table[1:2], 1, keepdims=True)
    skip = skip_ref[...].reshape(1, 256)
    base = keep * noisy_m[...].astype(F32) + gain * (jnp.concatenate([skip] * 4, 1) * pixels)
    i = iota((256, 256), 0)
    r, c = i >> 3, i & 7
    block = r >> 3
    spot = jnp.where((block == 1) | (block == 2), block - 1, jnp.where(block == third, 2, 3))
    source = (2 * (r & 1) + (c & 1)) * 64 + spot * 16 + ((r >> 1) & 3) * 4 + (c >> 1)
    unshuffle = (iota((256, 256), 1) == source).astype(F32).astype(BF)
    arrive(wo.at[near_blocks, 1 - core], w4_r.at[0], w4_s.at[0])
    arrive(wo.at[far_blocks, 1 - core], w4_r.at[1], w4_s.at[1])
    for d in range(8):

        @pl.when(there[d])
        def _():
            halo_copy(d).wait_send()

    wait_sent()

    coarse_next = pixels
    for turn in range(4):
        arrive(ret_r.at[turn], back_r.at[turn], back_s.at[0])
        first, second, weight = [], [], []
        for side in range(2):
            even, odd = ret_r[turn, 2 * side].astype(F32), ret_r[turn, 2 * side + 1].astype(F32)
            first.append(jnp.where(low, even, pltpu.roll(odd, 64, 1)))
            second.append(jnp.where(low, pltpu.roll(even, 64, 1), odd))
            weight.append(wo[side * 4 + (xx + 4 - turns[turn]) % 4].reshape(128, WIDE))
        heads = jnp.concatenate([jnp.concatenate(first, 1), jnp.concatenate(second, 1)], 0).astype(BF)
        coarse_next = coarse_next + mm(heads, jnp.concatenate(weight, 0))
    upsampled = mm(coarse_next.astype(BF), wup[...])
    sent_by(back_s.at[0], ret_s)
    wait_sent()
    result = base + gain * upsampled
    stacked = jnp.concatenate([result[:, ab * 256 : ab * 256 + 256] for ab in range(4)], 0)
    upper = stacked.astype(BF)
    lower = (stacked - upper.astype(F32)).astype(BF)
    out_ref[...] = (mm(unshuffle, upper) + mm(unshuffle, lower)).reshape(32, 8, 256)


def shards(
    noisy_image,
    time_index,
    solver_index,
    time_gains,
    pixel_qkv,
    pixel_out,
    coarse_gains,
    coarse_qkv,
    coarse_out,
    upsample_weight,
    skip_gain,
    solver_table,
):
    vmem = pl.BlockSpec(memory_space=pltpu.VMEM)
    smem = pl.BlockSpec(memory_space=pltpu.SMEM)
    hbm = pl.BlockSpec(memory_space=pltpu.HBM)
    dma = pltpu.SemaphoreType.DMA
    return pl.pallas_call(
        kernel,
        out_shape=jax.ShapeDtypeStruct((32, 8, 256), F32),
        in_specs=[smem] * 2 + [hbm] * 10,
        out_specs=vmem,
        scratch_shapes=[
            pltpu.VMEM((32, 8, 256), BF),
            pltpu.VMEM((2, 32), F32),
            pltpu.VMEM((32, 256), F32),
            pltpu.VMEM((256, 768), BF),
            pltpu.VMEM((256, 256), BF),
            pltpu.VMEM((32, WIDE), F32),
            pltpu.VMEM((256,), F32),
            pltpu.VMEM((320, 256), BF),
            pltpu.VMEM((160, 256), BF),
            pltpu.VMEM((160, 256), BF),
            pltpu.VMEM((128, 256), BF),
            pltpu.VMEM((128, 256), BF),
            pltpu.VMEM((320, 512), BF),
            pltpu.VMEM((320, 512), BF),
            pltpu.VMEM((256, 256), BF),
            pltpu.VMEM((64, WIDE), BF),
            pltpu.VMEM((64, WIDE), BF),
            pltpu.VMEM((64, WIDE), BF),
            pltpu.VMEM((2, 4, 2, 64, WIDE), BF),
            pltpu.VMEM((192, WIDE), BF),
            pltpu.VMEM((256, WIDE), BF),
            pltpu.VMEM((8, 2, 64, WIDE), BF),
            pltpu.VMEM((WIDE, WIDE), BF),
            pltpu.VMEM((2, 4, 2, 64, 128), BF),
            pltpu.VMEM((2, 4, 2, 64, 128), BF),
            pltpu.VMEM((2, 4, 2, 64, 128), BF),
            pltpu.VMEM((4, 4, 32, 128), BF),
            pltpu.VMEM((4, 4, 32, 128), BF),
            dma((8,)),
            dma((8,)),
            dma((2,)),
            dma((CHUNKS,)),
            dma((1,)),
            dma((CHUNKS,)),
            dma((1,)),
            dma((CHUNKS,)),
            dma((2,)),
            dma((CHUNKS,)),
            dma((1,)),
            dma((CHUNKS,)),
            dma((1,)),
            dma((1,)),
            dma((1,)),
            dma((1,)),
            dma((1,)),
            dma((1,)),
            dma((1,)),
            dma((1,)),
            dma((2,)),
            dma((2,)),
            dma((1,)),
            dma((4,)),
            dma((10,)),
        ],
        compiler_params=pltpu.CompilerParams(
            collective_id=0, has_side_effects=True, vmem_limit_bytes=48 * 1024 * 1024
        ),
        cost_estimate=pl.CostEstimate(flops=2_000_000_000, bytes_accessed=8_000_000, transcendentals=1_300_000),
    )(
        time_index,
        solver_index,
        *(
            pltpu.with_memory_space_constraint(array, pltpu.HBM)
            for array in (
                noisy_image,
                solver_table.T,
                time_gains,
                pixel_qkv,
                pixel_out,
                coarse_gains,
                skip_gain,
                coarse_qkv.reshape(coarse_qkv.shape[0], coarse_qkv.shape[2]).T,
                coarse_out,
                upsample_weight,
            )
        ),
    )


def solution(mesh):
    placed = (
        P("row", "col", None),
        P(),
        P(),
        P(),
        P(),
        P(),
        P(),
        P(None, "row", None),
        P("row", None),
        P(),
        P(),
        P(),
    )
    return jax.shard_map(
        shards, mesh=mesh, in_specs=placed, out_specs=P("row", "col", None), check_vma=False
    )
```

```python
import jax
import jax.numpy as jnp
from jax import lax
from jax.experimental import pallas as pl
from jax.experimental.pallas import tpu as pltpu
from jax.sharding import PartitionSpec as P

MESH = pl.DeviceIdType.MESH
BF = jnp.bfloat16
F32 = jnp.float32
ROWS, COLS = 16, 32
TOKENS = 64
WIDE = 1024
CHUNKS = 4
PER = TOKENS // CHUNKS
DIRS = ((-1, 0), (1, 0), (0, -1), (0, 1), (-1, -1), (-1, 1), (1, -1), (1, 1))


def iota(shape, dim):
    return lax.broadcasted_iota(jnp.int32, shape, dim)


def nt(left, right):
    return lax.dot_general(left, right, (((1,), (1,)), ((), ())), preferred_element_type=F32)


def mm(left, right):
    return jnp.dot(left, right, preferred_element_type=F32)


def norm(floats, scales):
    factor = lax.rsqrt(jnp.mean(floats * floats, -1, keepdims=True) + 1e-06)
    return (floats * factor * scales).astype(BF)


def pick(table, index):
    hit = iota(table.shape, 0) == index
    return jnp.sum(jnp.where(hit, table, 0.0), 0, keepdims=True)


def kernel(
    time_ref,
    step_ref,
    noisy_hbm,
    solver_hbm,
    gains_hbm,
    qkv_hbm,
    pout_hbm,
    cgains_hbm,
    skip_hbm,
    cqkv_hbm,
    cout_hbm,
    up_hbm,
    out_ref,
    noisy_ref,
    solver_ref,
    gains_ref,
    qkv_ref,
    pout_ref,
    cgains_ref,
    skip_ref,
    cc,
    ll,
    rr,
    pack_l,
    pack_r,
    kv_c,
    kv_e,
    query,
    noisy_m,
    merged,
    own,
    tok,
    wt,
    wt_other,
    w3,
    wo,
    wup,
    asked_all,
    keys_all,
    values_all,
    proj_s,
    proj_r,
    ret_s,
    ret_r,
    share_s,
    share_r,
    halo_s,
    halo_r,
    z_s,
    z_r,
    xr_s,
    xr_r,
    xl_s,
    xl_r,
    xf_s,
    xf_r,
    sib_s,
    sib_r,
    w1_s,
    w1_r,
    wx_s,
    wx_r,
    w2_s,
    w2_r,
    w3_s,
    w3_r,
    wt_s,
    wt_r,
    share_sems,
    back_s,
    back_r,
    local,
):
    row, col = lax.axis_index("row"), lax.axis_index("col")
    half, xx, core = row >> 3, (row >> 1) & 3, row & 1
    yy = col & 3
    group = row >> 1
    far_col = (col + 16) & 31
    far_row = (row + 8) & 15
    sibling = row + 1 - 2 * core

    fourth = jnp.where(row == 8, 0, 3)
    third = 3 - fourth

    def x_row(shift):
        return half * 8 + ((xx + shift) & 3) * 2 + core

    def y_col(shift):
        return col - yy + ((yy + shift) & 3)

    def remote(src, dst, send, recv, where):
        return pltpu.make_async_remote_copy(
            src_ref=src, dst_ref=dst, send_sem=send, recv_sem=recv, device_id=where, device_id_type=MESH
        )

    def arrive(dst, recv, send):
        remote(dst, dst, send, recv, (row, col)).wait_recv()

    sent = []

    def send(*args):
        remote(*args).start()

    def sent_by(sem, ref):
        sent.append((sem, ref))

    def wait_sent():
        for sem, ref in sent:
            remote(ref, ref, sem, local.at[0], (row, col)).wait_send()
        sent.clear()

    def load(src, dst, at):
        copy = pltpu.make_async_copy(src, dst, local.at[at])
        copy.start()
        return copy

    load_noisy = load(noisy_hbm, noisy_ref, 3)

    barrier = pltpu.get_barrier_semaphore()

    def greet(where):
        pl.semaphore_signal(barrier, inc=1, device_id=where, device_id_type=MESH)

    there = []
    for down, right in DIRS:
        r, c = row + down, col + right
        there.append((r >= 0) & (r < ROWS) & (c >= 0) & (c < COLS))
    for d, (down, right) in enumerate(DIRS):

        @pl.when(there[d])
        def _():
            greet((row + down, col + right))

    greet((row, far_col))
    greet((far_row, far_col))
    for shift in (1, 2, 3):
        greet((x_row(shift), col))
        greet((row, y_col(shift)))
    greet((sibling, col))
    partners = 2 + 6 + 1
    for flag in there:
        partners = partners + flag.astype(jnp.int32)

    quarter = pl.ds(pl.multiple_of(yy * 16, 16), 16)
    own_quarter = wo.at[group, quarter]
    own_block = wo.at[group]
    load_wo = load(cout_hbm, own_block, 0)
    load_gains = load(gains_hbm, gains_ref, 4)
    load_qkv = load(qkv_hbm, qkv_ref, 5)

    load_noisy.wait()
    tile = noisy_ref[...].astype(F32).reshape(256, 256)
    tile_b = tile.astype(BF)
    cc[32:288, :] = tile_b
    spot = iota((128, 256), 0)
    place = (spot >> 2) * 8 + (spot & 3)
    lane = iota((128, 256), 1)
    pack_l[...] = mm((lane == place).astype(F32).astype(BF), tile_b).astype(BF)
    pack_r[...] = mm((lane == place + 4).astype(F32).astype(BF), tile_b).astype(BF)

    pl.semaphore_wait(barrier, partners)

    halo = (
        (cc.at[32:64], cc.at[288:320]),
        (cc.at[256:288], cc.at[0:32]),
        (pack_l, rr.at[16:144]),
        (pack_r, ll.at[16:144]),
        (pack_l.at[0:16], rr.at[144:160]),
        (pack_r.at[0:16], ll.at[144:160]),
        (pack_l.at[112:128], rr.at[0:16]),
        (pack_r.at[112:128], ll.at[0:16]),
    )

    def halo_copy(d):
        src, dst = halo[d]
        return remote(src, dst, halo_s.at[d], halo_r.at[d], (row + DIRS[d][0], col + DIRS[d][1]))

    for d in (2, 3, 0, 1, 4, 5, 6, 7):

        @pl.when(there[d])
        def _():
            halo_copy(d).start()

    from_there = []
    for down, right in DIRS:
        r, c = row - down, col - right
        from_there.append((r >= 0) & (r < ROWS) & (c >= 0) & (c < COLS))
    for d in range(8):

        @pl.when(jnp.logical_not(from_there[d]))
        def _():
            dst = halo[d][1]
            dst[...] = jnp.zeros(dst.shape, BF)

    load_pout = load(pout_hbm, pout_ref, 6)
    load_cgains = load(cgains_hbm, cgains_ref, 7)
    load_wt = load(cqkv_hbm, wt, 1)
    load_skip = load(skip_hbm, skip_ref, 8)
    load_solver = load(solver_hbm, solver_ref, 9)
    load_up = load(up_hbm, wup, 2)

    load_wo.wait()
    send(own_quarter, own_quarter, w1_s.at[0], w1_r.at[0], (far_row, far_col))
    sent_by(w1_s.at[0], own_quarter)
    three = pl.ds(0, 3)
    for shift in (1, 2, 3):
        send(own_block, own_block, wx_s.at[0], wx_r.at[0], (x_row(shift), col))
    sent_by(wx_s.at[0], wo.at[three])

    load_gains.wait()
    scales = pick(gains_ref[...], time_ref[0])
    normed = norm(tile, scales)
    load_qkv.wait()
    kv_c[32:288, :] = mm(normed, qkv_ref[:, 256:768]).astype(BF)
    i = iota((256, 256), 0)
    spot, a, b, p, q = i >> 6, (i >> 5) & 1, (i >> 4) & 1, (i >> 2) & 3, i & 3
    blk = jnp.where(spot < 2, spot + 1, jnp.where(spot == 2, third, fourth))
    source = (8 * blk + 2 * p + a) * 8 + 2 * q + b
    shuffle = (iota((256, 256), 1) == source).astype(F32).astype(BF)
    noisy_q = mm(shuffle, tile_b)
    normed_q = mm(shuffle, normed).astype(BF)
    query[...] = mm(normed_q, qkv_ref[:, 0:256]).astype(BF)
    noisy_qb = noisy_q.astype(BF)
    for block in range(4):
        for ab in range(4):
            at = block * 64 + ab * 16
            noisy_m[block * 16 : block * 16 + 16, ab * 256 : ab * 256 + 256] = noisy_qb[at : at + 16]

    load_wt.wait()
    send(wt, wt_other, wt_s.at[0], wt_r.at[0], (sibling, col))
    sent_by(wt_s.at[0], wt)
    w3[0:64, :] = (wt[0:64, :].astype(F32) * 0.125).astype(BF)
    w3[64:192, :] = wt[64:192, :]
    w3[192:256, :] = jnp.zeros((64, WIDE), BF)

    def halo_wait(d, flag):
        @pl.when(from_there[d] & flag)
        def _():
            arrive(halo[d][1], halo_r.at[d], halo_s.at[d])

    def edge_kv(array):
        return mm(norm(array.astype(F32), scales), qkv_ref[:, 256:768]).astype(BF)

    halo_wait(2, True)
    halo_wait(3, True)
    sides = edge_kv(jnp.concatenate([ll[16:144, :], rr[16:144, :]], 0))
    kv_e[16:144, :] = sides[0:128]
    kv_e[176:304, :] = sides[128:256]

    def outer_edge(block, last):
        above = (row == 8) if last else (row != 8)
        for d in (1, 6, 7):
            halo_wait(d, above)
        for d in (0, 4, 5):
            halo_wait(d, jnp.logical_not(above))
        wide = pl.ds(pl.multiple_of(jnp.where(block == 0, 0, 288), 32), 32)
        start = jnp.where(block == 0, 0, 144)
        narrow = pl.ds(pl.multiple_of(start, 16), 16)
        result = edge_kv(jnp.concatenate([cc[wide, :], ll[narrow, :], rr[narrow, :]], 0))
        kv_c[wide, :] = result[0:32]
        kv_e[narrow, :] = result[32:48]
        kv_e[pl.ds(pl.multiple_of(160 + start, 16), 16), :] = result[48:64]

    j = iota((64, 256), 1)
    in_c = j < 128
    key_row = jnp.where(in_c, j >> 3, (j & 63) >> 2) - 4
    key_col = jnp.where(in_c, j & 7, (j & 3) + jnp.where(j < 192, -4, 8))
    i = iota((64, 256), 0)
    query_row = 2 * ((i >> 2) & 3) + ((i >> 5) & 1)
    query_col = 2 * (i & 3) + ((i >> 4) & 1)
    full_col = key_col + col * 8
    near = (
        (jnp.abs(key_row - query_row) <= 3)
        & (jnp.abs(key_col - query_col) <= 3)
        & (full_col >= 0)
        & (full_col < 256)
    )
    head_of = iota((64, 256), 1) >> 6
    ones = jnp.ones((256, 256), BF)
    load_cgains.wait()
    load_pout.wait()
    coarse_scales = pick(cgains_ref[...], time_ref[0])

    def window_block(spot, block):
        inner = pl.ds(pl.multiple_of(64 * block, 64), 128)
        lefts = pl.ds(pl.multiple_of(32 * block, 32), 64)
        rights = pl.ds(pl.multiple_of(160 + 32 * block, 32), 64)
        keys = jnp.concatenate([kv_c[inner, 0:256], kv_e[lefts, 0:256], kv_e[rights, 0:256]], 0)
        values = jnp.concatenate([kv_c[inner, 256:512], kv_e[lefts, 256:512], kv_e[rights, 256:512]], 0)
        asked = query[64 * spot : 64 * spot + 64, :].astype(F32) * 0.125
        spread = jnp.concatenate([jnp.where(head_of == h, asked, 0.0) for h in range(4)], 0).astype(BF)
        full_row = key_row + (row * 32 + 8 * block)
        usable = near & (full_row >= 0) & (full_row < 512)
        bias = jnp.where(usable, 0.0, -1e30)
        scores = nt(spread, keys) + jnp.concatenate([bias] * 4, 0)
        weights = jnp.exp(scores - jnp.max(scores, 1, keepdims=True)).astype(BF)
        sums = mm(weights, ones)
        mixed = mm(weights, values)
        total, share = jnp.zeros((64, 256), F32), jnp.zeros((64, 256), F32)
        for h in range(4):
            total = jnp.where(head_of == h, sums[64 * h : 64 * h + 64], total)
            share = jnp.where(head_of == h, mixed[64 * h : 64 * h + 64], share)
        attended = (share / total).astype(BF)
        delta = mm(attended, pout_ref[...])
        for ab in range(4):
            rows, lanes = pl.ds(spot * 16, 16), pl.ds(ab * 256, 256)
            pixels = noisy_m[rows, lanes].astype(F32) + delta[ab * 16 : ab * 16 + 16]
            merged[rows, lanes] = pixels.astype(BF)

    def part(k):
        return pl.ds(k * PER, PER)

    far_blocks = pl.ds(pl.multiple_of(4 - half * 4, 4), 4)

    def weights_x():
        ref = wo.at[far_row >> 1, quarter]
        arrive(ref, w1_r.at[0], w1_s.at[0])
        for shift in (1, 2, 3):
            send(ref, ref, w2_s.at[0], w2_r.at[0], (x_row(shift), col))
        sent_by(w2_s.at[0], wo.at[three, quarter])

    def weights_y():
        arrive(wo.at[three, quarter], w2_r.at[0], w2_s.at[0])
        ref = wo.at[far_blocks, quarter]
        for shift in (1, 2, 3):
            send(ref, ref, w3_s.at[0], w3_r.at[0], (row, y_col(shift)))
        sent_by(w3_s.at[0], wo.at[far_blocks, pl.ds(0, 48)])

    for k in range(CHUNKS):
        if k == 3:
            weights_x()
        if k < 2:
            window_block(k, k + 1)
        else:
            outer_edge(third if k == 2 else fourth, k == 3)
            window_block(k, third if k == 2 else fourth)
        own[part(k), :] = norm(merged[part(k), :].astype(F32), coarse_scales)
        for t, target in enumerate((row, far_row)):
            send(
                own.at[part(k)],
                tok.at[half, xx >> 1, xx & 1, part(k)],
                z_s.at[t],
                z_r.at[k],
                (target, far_col),
            )
    for t in range(2):
        sent_by(z_s.at[t], own)

    def blocks(shift, k):
        at = (xx + shift) & 3
        return tok.at[:, at >> 1, at & 1, part(k)]

    def one(side, shift, k):
        at = (xx + shift) & 3
        return tok.at[side, at >> 1, at & 1, part(k)]

    def gather(k):
        ref = blocks(0, k)
        arrive(ref, z_r.at[k], z_s.at[0])
        send(ref, ref, xr_s.at[0], xr_r.at[k], (x_row(1), col))
        send(ref, ref, xl_s.at[0], xl_r.at[k], (x_row(3), col))

    def relay(k):
        arrive(blocks(3, k), xr_r.at[k], xr_s.at[0])
        ref = one(0, 3, k)
        send(ref, ref, xf_s.at[0], xf_r.at[k], (x_row(1), col))
        arrive(blocks(1, k), xl_r.at[k], xl_s.at[0])
        ref = one(1, 1, k)
        send(ref, ref, xf_s.at[1], xf_r.at[k], (x_row(3), col))

    def finish(k):
        arrive(blocks(2, k), xf_r.at[k], xf_s.at[0])

    left = iota((8 * PER, 128), 1) < 64

    def keep_proj(result, which, k):
        both, value = result[:, 0:128], result[:, 128:256]
        for ref, array in (
            (asked_all, jnp.where(left, both, 0.0)),
            (keys_all, pltpu.roll(both, 64, 1)),
            (values_all, jnp.where(left, value, 1.0)),
        ):
            ref[:, :, which, k * PER : (k + 1) * PER, :] = array.astype(BF).reshape(2, 4, PER, 128)

    def project(k):
        tokens = tok[:, :, :, k * PER : (k + 1) * PER, :].reshape(8 * PER, WIDE)
        result = nt(tokens, w3[...])
        proj_s[k] = result[:, 256:512].astype(BF)
        send(proj_s.at[k], proj_r.at[k], sib_s.at[0], sib_r.at[k], (sibling, col))
        keep_proj(result[:, 0:256], core, k)

    def from_sibling(k):
        arrive(proj_r.at[k], sib_r.at[k], sib_s.at[0])
        keep_proj(proj_r[k].astype(F32), 1 - core, k)

    weights_y()
    arrive(wt_other, wt_r.at[0], wt_s.at[0])
    w3[256:320, :] = (wt_other[0:64, :].astype(F32) * 0.125).astype(BF)
    w3[320:448, :] = wt_other[64:192, :]
    w3[448:512, :] = jnp.zeros((64, WIDE), BF)

    gather(0)
    relay(0)
    for k in range(1, CHUNKS):
        gather(k)
        finish(k - 1)
        relay(k)
        project(k - 1)
        if k > 1:
            from_sibling(k - 2)
    finish(CHUNKS - 1)
    project(CHUNKS - 1)
    from_sibling(CHUNKS - 2)
    from_sibling(CHUNKS - 1)

    low = iota((32, 128), 1) < 64
    keys = keys_all[...].reshape(WIDE, 128)
    values = values_all[...].reshape(WIDE, 128)

    turns = (2, 1, 3, 0)

    def score(turn):
        return nt(asked_all[:, ((xx + turns[turn]) & 3)].reshape(256, 128), keys)

    for sem in (xr_s.at[0], xl_s.at[0]):
        sent_by(sem, tok.at[:, 0, 0])
    for side in range(2):
        sent_by(xf_s.at[side], tok.at[side, 0, 0])
    sent_by(sib_s.at[0], proj_s)

    scores = score(0)
    for turn in range(4):
        following = score(turn + 1) if turn < 3 else None
        weights = jnp.exp(scores - jnp.max(scores, 1, keepdims=True)).astype(BF)
        mixed = mm(weights, values)
        mixed = mixed / pltpu.roll(mixed, 64, 1)
        for which in range(4):
            at = 64 * which
            packed = jnp.where(low, mixed[at : at + 32], pltpu.roll(mixed[at + 32 : at + 64], 64, 1))
            ret_s[turn, which // 2, which % 2] = packed.astype(BF)
        for side in range(2):
            target = side * 8 + ((xx + turns[turn]) & 3) * 2 + core
            send(ret_s.at[turn, side], ret_r.at[turn, half], back_s.at[0], back_r.at[turn], (target, far_col))
        scores = following

    load_up.wait()
    load_skip.wait()
    load_solver.wait()
    pixels = merged[...].astype(F32)
    table = solver_ref[...]
    table = jnp.where(iota(table.shape, 1) == step_ref[0], table, 0.0)
    keep = jnp.sum(table[0:1], 1, keepdims=True)
    gain = jnp.sum(table[1:2], 1, keepdims=True)
    skip = skip_ref[...].reshape(1, 256)
    base = keep * noisy_m[...].astype(F32) + gain * (jnp.concatenate([skip] * 4, 1) * pixels)
    i = iota((256, 256), 0)
    r, c = i >> 3, i & 7
    block = r >> 3
    spot = jnp.where((block == 1) | (block == 2), block - 1, jnp.where(block == third, 2, 3))
    source = (2 * (r & 1) + (c & 1)) * 64 + spot * 16 + ((r >> 1) & 3) * 4 + (c >> 1)
    unshuffle = (iota((256, 256), 1) == source).astype(F32).astype(BF)
    arrive(wo.at[three], wx_r.at[0], wx_s.at[0])
    arrive(wo.at[far_blocks, pl.ds(0, 48)], w3_r.at[0], w3_s.at[0])
    for d in range(8):

        @pl.when(there[d])
        def _():
            halo_copy(d).wait_send()

    wait_sent()

    def head_rows(turn, which):
        even, odd = ret_r[turn, 0, which].astype(F32), ret_r[turn, 1, which].astype(F32)
        first = jnp.where(low, even, pltpu.roll(odd, 64, 1))
        second = jnp.where(low, pltpu.roll(even, 64, 1), odd)
        return jnp.concatenate([first, second], 0).astype(BF)

    shares = [None, None]
    for couple in range(2):
        weight = []
        for turn in (2 * couple, 2 * couple + 1):
            arrive(ret_r.at[turn], back_r.at[turn], back_s.at[0])
            from_x = (xx + 4 - turns[turn]) & 3
            weight += [wo[from_x], wo[4 + from_x]]
        weight = jnp.concatenate(weight, 0)
        for at, which in enumerate((1 - core, core)):
            heads = jnp.concatenate([head_rows(2 * couple, which), head_rows(2 * couple + 1, which)], 1)
            share = mm(heads, weight)
            shares[at] = share if couple == 0 else shares[at] + share
            if couple == 1 and at == 0:
                share_s[...] = shares[0].astype(BF)
                send(share_s, share_r, share_sems.at[0], share_sems.at[1], (sibling, col))
    coarse_next = pixels + shares[1]
    arrive(share_r, share_sems.at[1], share_sems.at[0])
    coarse_next = coarse_next + share_r[...].astype(F32)
    upsampled = mm(coarse_next.astype(BF), wup[...])
    sent_by(back_s.at[0], ret_s)
    sent_by(share_sems.at[0], share_s)
    wait_sent()
    result = base + gain * upsampled
    stacked = jnp.concatenate([result[:, ab * 256 : ab * 256 + 256] for ab in range(4)], 0)
    upper = stacked.astype(BF)
    lower = (stacked - upper.astype(F32)).astype(BF)
    out_ref[...] = (mm(unshuffle, upper) + mm(unshuffle, lower)).reshape(32, 8, 256)


def shards(
    noisy_image,
    time_index,
    solver_index,
    time_gains,
    pixel_qkv,
    pixel_out,
    coarse_gains,
    coarse_qkv,
    coarse_out,
    upsample_weight,
    skip_gain,
    solver_table,
):
    vmem = pl.BlockSpec(memory_space=pltpu.VMEM)
    smem = pl.BlockSpec(memory_space=pltpu.SMEM)
    hbm = pl.BlockSpec(memory_space=pltpu.HBM)
    dma = pltpu.SemaphoreType.DMA
    return pl.pallas_call(
        kernel,
        out_shape=jax.ShapeDtypeStruct((32, 8, 256), F32),
        in_specs=[smem] * 2 + [hbm] * 10,
        out_specs=vmem,
        scratch_shapes=[
            pltpu.VMEM((32, 8, 256), BF),
            pltpu.VMEM((2, 32), F32),
            pltpu.VMEM((32, 256), F32),
            pltpu.VMEM((256, 768), BF),
            pltpu.VMEM((256, 256), BF),
            pltpu.VMEM((32, WIDE), F32),
            pltpu.VMEM((256,), F32),
            pltpu.VMEM((320, 256), BF),
            pltpu.VMEM((160, 256), BF),
            pltpu.VMEM((160, 256), BF),
            pltpu.VMEM((128, 256), BF),
            pltpu.VMEM((128, 256), BF),
            pltpu.VMEM((320, 512), BF),
            pltpu.VMEM((320, 512), BF),
            pltpu.VMEM((256, 256), BF),
            pltpu.VMEM((64, WIDE), BF),
            pltpu.VMEM((64, WIDE), BF),
            pltpu.VMEM((64, WIDE), BF),
            pltpu.VMEM((2, 2, 2, 64, WIDE), BF),
            pltpu.VMEM((192, WIDE), BF),
            pltpu.VMEM((192, WIDE), BF),
            pltpu.VMEM((512, WIDE), BF),
            pltpu.VMEM((8, 64, WIDE), BF),
            pltpu.VMEM((WIDE, WIDE), BF),
            pltpu.VMEM((2, 4, 2, 64, 128), BF),
            pltpu.VMEM((2, 4, 2, 64, 128), BF),
            pltpu.VMEM((2, 4, 2, 64, 128), BF),
            pltpu.VMEM((CHUNKS, 8 * PER, 256), BF),
            pltpu.VMEM((CHUNKS, 8 * PER, 256), BF),
            pltpu.VMEM((4, 2, 2, 32, 128), BF),
            pltpu.VMEM((4, 2, 2, 32, 128), BF),
            pltpu.VMEM((64, WIDE), BF),
            pltpu.VMEM((64, WIDE), BF),
            dma((8,)),
            dma((8,)),
            dma((2,)),
            dma((CHUNKS,)),
            dma((1,)),
            dma((CHUNKS,)),
            dma((1,)),
            dma((CHUNKS,)),
            dma((2,)),
            dma((CHUNKS,)),
            dma((1,)),
            dma((CHUNKS,)),
            dma((1,)),
            dma((1,)),
            dma((1,)),
            dma((1,)),
            dma((1,)),
            dma((1,)),
            dma((1,)),
            dma((1,)),
            dma((1,)),
            dma((1,)),
            dma((2,)),
            dma((1,)),
            dma((4,)),
            dma((10,)),
        ],
        compiler_params=pltpu.CompilerParams(
            collective_id=0, has_side_effects=True, vmem_limit_bytes=48 * 1024 * 1024
        ),
        cost_estimate=pl.CostEstimate(flops=2_000_000_000, bytes_accessed=8_000_000, transcendentals=1_300_000),
    )(
        time_index,
        solver_index,
        *(
            pltpu.with_memory_space_constraint(array, pltpu.HBM)
            for array in (
                noisy_image,
                solver_table.T,
                time_gains,
                pixel_qkv,
                pixel_out,
                coarse_gains,
                skip_gain,
                coarse_qkv.reshape(coarse_qkv.shape[0], coarse_qkv.shape[2]).T,
                coarse_out,
                upsample_weight,
            )
        ),
    )


def solution(mesh):
    placed = (
        P("row", "col", None),
        P(),
        P(),
        P(),
        P(),
        P(),
        P(),
        P(None, "row", None),
        P("row", None),
        P(),
        P(),
        P(),
    )
    return jax.shard_map(
        shards, mesh=mesh, in_specs=placed, out_specs=P("row", "col", None), check_vma=False
    )
```

```python
import jax
import jax.numpy as jnp
from jax import lax
from jax.experimental import pallas as pl
from jax.experimental.pallas import tpu as pltpu
from jax.sharding import PartitionSpec as P

MESH = pl.DeviceIdType.MESH
BF = jnp.bfloat16
F32 = jnp.float32
ROWS, COLS = 16, 32
TOKENS = 64
WIDE = 1024
CHUNKS = 4
PER = TOKENS // CHUNKS
DIRS = ((-1, 0), (1, 0), (0, -1), (0, 1), (-1, -1), (-1, 1), (1, -1), (1, 1))


def iota(shape, dim):
    return lax.broadcasted_iota(jnp.int32, shape, dim)


def nt(left, right):
    return lax.dot_general(left, right, (((1,), (1,)), ((), ())), preferred_element_type=F32)


def mm(left, right):
    return jnp.dot(left, right, preferred_element_type=F32)


def norm(floats, scales):
    factor = lax.rsqrt(jnp.mean(floats * floats, -1, keepdims=True) + 1e-06)
    return (floats * factor * scales).astype(BF)


def pick(table, index):
    hit = iota(table.shape, 0) == index
    return jnp.sum(jnp.where(hit, table, 0.0), 0, keepdims=True)


def kernel(
    time_ref,
    step_ref,
    noisy_hbm,
    solver_hbm,
    gains_hbm,
    qkv_hbm,
    pout_hbm,
    cgains_hbm,
    skip_hbm,
    cqkv_hbm,
    cout_hbm,
    up_hbm,
    out_ref,
    noisy_ref,
    solver_ref,
    gains_ref,
    qkv_ref,
    pout_ref,
    cgains_ref,
    skip_ref,
    cc,
    ll,
    rr,
    pack_l,
    pack_r,
    kv_c,
    kv_e,
    query,
    noisy_m,
    merged,
    own,
    tok,
    wt,
    wt_other,
    w3,
    wo,
    wup,
    asked_all,
    keys_all,
    values_all,
    proj_s,
    proj_r,
    ret_s,
    ret_r,
    share_s,
    share_r,
    halo_s,
    halo_r,
    z_s,
    z_r,
    xr_s,
    xr_r,
    xl_s,
    xl_r,
    xf_s,
    xf_r,
    sib_s,
    sib_r,
    w1_s,
    w1_r,
    w2_s,
    w2_r,
    w3_s,
    w3_r,
    wt_s,
    wt_r,
    share_sems,
    back_s,
    back_r,
    local,
):
    row, col = lax.axis_index("row"), lax.axis_index("col")
    half, xx, core = row >> 3, (row >> 1) & 3, row & 1
    yy = col & 3
    group = row >> 1
    far_col = (col + 16) & 31
    far_row = (row + 8) & 15
    sibling = row + 1 - 2 * core

    fourth = jnp.where(row == 8, 0, 3)
    third = 3 - fourth

    def x_row(shift):
        return half * 8 + ((xx + shift) & 3) * 2 + core

    def y_col(shift):
        return col - yy + ((yy + shift) & 3)

    def remote(src, dst, send, recv, where):
        return pltpu.make_async_remote_copy(
            src_ref=src, dst_ref=dst, send_sem=send, recv_sem=recv, device_id=where, device_id_type=MESH
        )

    def arrive(dst, recv, send):
        remote(dst, dst, send, recv, (row, col)).wait_recv()

    sent = []

    def send(*args):
        remote(*args).start()

    def sent_by(sem, ref):
        sent.append((sem, ref))

    def wait_sent():
        for sem, ref in sent:
            remote(ref, ref, sem, local.at[0], (row, col)).wait_send()
        sent.clear()

    def load(src, dst, at):
        copy = pltpu.make_async_copy(src, dst, local.at[at])
        copy.start()
        return copy

    load_noisy = load(noisy_hbm, noisy_ref, 3)

    barrier = pltpu.get_barrier_semaphore()

    def greet(where):
        pl.semaphore_signal(barrier, inc=1, device_id=where, device_id_type=MESH)

    there = []
    for down, right in DIRS:
        r, c = row + down, col + right
        there.append((r >= 0) & (r < ROWS) & (c >= 0) & (c < COLS))
    for d, (down, right) in enumerate(DIRS):

        @pl.when(there[d])
        def _():
            greet((row + down, col + right))

    greet((row, far_col))
    greet((far_row, far_col))
    for shift in (1, 2, 3):
        greet((x_row(shift), col))
        greet((row, y_col(shift)))
    greet((sibling, col))
    partners = 2 + 6 + 1
    for flag in there:
        partners = partners + flag.astype(jnp.int32)

    quarter = pl.ds(pl.multiple_of(yy * 16, 16), 16)
    own_quarter = wo.at[group, quarter]
    load_wo = load(cout_hbm.at[quarter], own_quarter, 0)
    load_gains = load(gains_hbm, gains_ref, 4)
    load_qkv = load(qkv_hbm, qkv_ref, 5)

    load_noisy.wait()
    tile = noisy_ref[...].astype(F32).reshape(256, 256)
    tile_b = tile.astype(BF)
    cc[32:288, :] = tile_b
    spot = iota((128, 256), 0)
    place = (spot >> 2) * 8 + (spot & 3)
    lane = iota((128, 256), 1)
    pack_l[...] = mm((lane == place).astype(F32).astype(BF), tile_b).astype(BF)
    pack_r[...] = mm((lane == place + 4).astype(F32).astype(BF), tile_b).astype(BF)

    pl.semaphore_wait(barrier, partners)

    halo = (
        (cc.at[32:64], cc.at[288:320]),
        (cc.at[256:288], cc.at[0:32]),
        (pack_l, rr.at[16:144]),
        (pack_r, ll.at[16:144]),
        (pack_l.at[0:16], rr.at[144:160]),
        (pack_r.at[0:16], ll.at[144:160]),
        (pack_l.at[112:128], rr.at[0:16]),
        (pack_r.at[112:128], ll.at[0:16]),
    )

    def halo_copy(d):
        src, dst = halo[d]
        return remote(src, dst, halo_s.at[d], halo_r.at[d], (row + DIRS[d][0], col + DIRS[d][1]))

    for d in (2, 3, 0, 1, 4, 5, 6, 7):

        @pl.when(there[d])
        def _():
            halo_copy(d).start()

    from_there = []
    for down, right in DIRS:
        r, c = row - down, col - right
        from_there.append((r >= 0) & (r < ROWS) & (c >= 0) & (c < COLS))
    for d in range(8):

        @pl.when(jnp.logical_not(from_there[d]))
        def _():
            dst = halo[d][1]
            dst[...] = jnp.zeros(dst.shape, BF)

    load_pout = load(pout_hbm, pout_ref, 6)
    load_cgains = load(cgains_hbm, cgains_ref, 7)
    load_wt = load(cqkv_hbm, wt, 1)
    load_skip = load(skip_hbm, skip_ref, 8)
    load_solver = load(solver_hbm, solver_ref, 9)
    load_up = load(up_hbm, wup, 2)

    load_wo.wait()
    send(own_quarter, own_quarter, w1_s.at[0], w1_r.at[0], (far_row, far_col))
    sent_by(w1_s.at[0], own_quarter)
    three = pl.ds(0, 3)
    for shift in (1, 2, 3):
        send(own_quarter, own_quarter, w2_s.at[0], w2_r.at[0], (x_row(shift), col))

    load_gains.wait()
    scales = pick(gains_ref[...], time_ref[0])
    normed = norm(tile, scales)
    load_qkv.wait()
    kv_c[32:288, :] = mm(normed, qkv_ref[:, 256:768]).astype(BF)
    i = iota((256, 256), 0)
    spot, a, b, p, q = i >> 6, (i >> 5) & 1, (i >> 4) & 1, (i >> 2) & 3, i & 3
    blk = jnp.where(spot < 2, spot + 1, jnp.where(spot == 2, third, fourth))
    source = (8 * blk + 2 * p + a) * 8 + 2 * q + b
    shuffle = (iota((256, 256), 1) == source).astype(F32).astype(BF)
    noisy_q = mm(shuffle, tile_b)
    normed_q = mm(shuffle, normed).astype(BF)
    query[...] = mm(normed_q, qkv_ref[:, 0:256]).astype(BF)
    noisy_qb = noisy_q.astype(BF)
    for block in range(4):
        for ab in range(4):
            at = block * 64 + ab * 16
            noisy_m[block * 16 : block * 16 + 16, ab * 256 : ab * 256 + 256] = noisy_qb[at : at + 16]

    load_wt.wait()
    send(wt, wt_other, wt_s.at[0], wt_r.at[0], (sibling, col))
    sent_by(wt_s.at[0], wt)
    w3[0:64, :] = (wt[0:64, :].astype(F32) * 0.125).astype(BF)
    w3[64:192, :] = wt[64:192, :]
    w3[192:256, :] = jnp.zeros((64, WIDE), BF)

    def halo_wait(d, flag):
        @pl.when(from_there[d] & flag)
        def _():
            arrive(halo[d][1], halo_r.at[d], halo_s.at[d])

    def edge_kv(array):
        return mm(norm(array.astype(F32), scales), qkv_ref[:, 256:768]).astype(BF)

    halo_wait(2, True)
    halo_wait(3, True)
    sides = edge_kv(jnp.concatenate([ll[16:144, :], rr[16:144, :]], 0))
    kv_e[16:144, :] = sides[0:128]
    kv_e[176:304, :] = sides[128:256]

    def outer_edge(block, last):
        above = (row == 8) if last else (row != 8)
        for d in (1, 6, 7):
            halo_wait(d, above)
        for d in (0, 4, 5):
            halo_wait(d, jnp.logical_not(above))
        wide = pl.ds(pl.multiple_of(jnp.where(block == 0, 0, 288), 32), 32)
        start = jnp.where(block == 0, 0, 144)
        narrow = pl.ds(pl.multiple_of(start, 16), 16)
        result = edge_kv(jnp.concatenate([cc[wide, :], ll[narrow, :], rr[narrow, :]], 0))
        kv_c[wide, :] = result[0:32]
        kv_e[narrow, :] = result[32:48]
        kv_e[pl.ds(pl.multiple_of(160 + start, 16), 16), :] = result[48:64]

    j = iota((64, 256), 1)
    in_c = j < 128
    key_row = jnp.where(in_c, j >> 3, (j & 63) >> 2) - 4
    key_col = jnp.where(in_c, j & 7, (j & 3) + jnp.where(j < 192, -4, 8))
    i = iota((64, 256), 0)
    query_row = 2 * ((i >> 2) & 3) + ((i >> 5) & 1)
    query_col = 2 * (i & 3) + ((i >> 4) & 1)
    full_col = key_col + col * 8
    near = (
        (jnp.abs(key_row - query_row) <= 3)
        & (jnp.abs(key_col - query_col) <= 3)
        & (full_col >= 0)
        & (full_col < 256)
    )
    head_of = iota((64, 256), 1) >> 6
    ones = jnp.ones((256, 256), BF)
    load_cgains.wait()
    load_pout.wait()
    coarse_scales = pick(cgains_ref[...], time_ref[0])

    def window_block(spot, block):
        inner = pl.ds(pl.multiple_of(64 * block, 64), 128)
        lefts = pl.ds(pl.multiple_of(32 * block, 32), 64)
        rights = pl.ds(pl.multiple_of(160 + 32 * block, 32), 64)
        keys = jnp.concatenate([kv_c[inner, 0:256], kv_e[lefts, 0:256], kv_e[rights, 0:256]], 0)
        values = jnp.concatenate([kv_c[inner, 256:512], kv_e[lefts, 256:512], kv_e[rights, 256:512]], 0)
        asked = query[64 * spot : 64 * spot + 64, :].astype(F32) * 0.125
        spread = jnp.concatenate([jnp.where(head_of == h, asked, 0.0) for h in range(4)], 0).astype(BF)
        full_row = key_row + (row * 32 + 8 * block)
        usable = near & (full_row >= 0) & (full_row < 512)
        bias = jnp.where(usable, 0.0, -1e30)
        scores = nt(spread, keys) + jnp.concatenate([bias] * 4, 0)
        weights = jnp.exp(scores - jnp.max(scores, 1, keepdims=True)).astype(BF)
        sums = mm(weights, ones)
        mixed = mm(weights, values)
        total, share = jnp.zeros((64, 256), F32), jnp.zeros((64, 256), F32)
        for h in range(4):
            total = jnp.where(head_of == h, sums[64 * h : 64 * h + 64], total)
            share = jnp.where(head_of == h, mixed[64 * h : 64 * h + 64], share)
        attended = (share / total).astype(BF)
        delta = mm(attended, pout_ref[...])
        for ab in range(4):
            rows, lanes = pl.ds(spot * 16, 16), pl.ds(ab * 256, 256)
            pixels = noisy_m[rows, lanes].astype(F32) + delta[ab * 16 : ab * 16 + 16]
            merged[rows, lanes] = pixels.astype(BF)

    def part(k):
        return pl.ds(k * PER, PER)

    def weights_x():
        ref = wo.at[far_row >> 1, quarter]
        arrive(ref, w1_r.at[0], w1_s.at[0])
        for shift in (1, 2, 3):
            send(ref, ref, w2_s.at[1], w2_r.at[1], (x_row(shift), col))

    def weights_y(far):
        arrive(wo.at[three, quarter], w2_r.at[far], w2_s.at[far])
        sent_by(w2_s.at[far], wo.at[three, quarter])
        side = 1 - half if far else half
        ref = wo.at[pl.ds(pl.multiple_of(side * 4, 4), 4), quarter]
        for shift in (1, 2, 3):
            send(ref, ref, w3_s.at[far], w3_r.at[far], (row, y_col(shift)))
        sent_by(w3_s.at[far], wo.at[pl.ds(0, 4), pl.ds(0, 48)])

    for k in range(CHUNKS):
        if k == 2:
            weights_y(0)
        if k == 3:
            weights_x()
        if k < 2:
            window_block(k, k + 1)
        else:
            outer_edge(third if k == 2 else fourth, k == 3)
            window_block(k, third if k == 2 else fourth)
        own[part(k), :] = norm(merged[part(k), :].astype(F32), coarse_scales)
        for t, target in enumerate((row, far_row)):
            send(
                own.at[part(k)],
                tok.at[half, xx >> 1, xx & 1, part(k)],
                z_s.at[t],
                z_r.at[k],
                (target, far_col),
            )
    for t in range(2):
        sent_by(z_s.at[t], own)

    def blocks(shift, k):
        at = (xx + shift) & 3
        return tok.at[:, at >> 1, at & 1, part(k)]

    def one(side, shift, k):
        at = (xx + shift) & 3
        return tok.at[side, at >> 1, at & 1, part(k)]

    def gather(k):
        ref = blocks(0, k)
        arrive(ref, z_r.at[k], z_s.at[0])
        send(ref, ref, xr_s.at[0], xr_r.at[k], (x_row(1), col))
        send(ref, ref, xl_s.at[0], xl_r.at[k], (x_row(3), col))

    def relay(k):
        arrive(blocks(3, k), xr_r.at[k], xr_s.at[0])
        ref = one(0, 3, k)
        send(ref, ref, xf_s.at[0], xf_r.at[k], (x_row(1), col))
        arrive(blocks(1, k), xl_r.at[k], xl_s.at[0])
        ref = one(1, 1, k)
        send(ref, ref, xf_s.at[1], xf_r.at[k], (x_row(3), col))

    def finish(k):
        arrive(blocks(2, k), xf_r.at[k], xf_s.at[0])

    left = iota((8 * PER, 128), 1) < 64

    def keep_proj(result, which, k):
        both, value = result[:, 0:128], result[:, 128:256]
        for ref, array in (
            (asked_all, jnp.where(left, both, 0.0)),
            (keys_all, pltpu.roll(both, 64, 1)),
            (values_all, jnp.where(left, value, 1.0)),
        ):
            ref[:, :, which, k * PER : (k + 1) * PER, :] = array.astype(BF).reshape(2, 4, PER, 128)

    def project(k):
        tokens = tok[:, :, :, k * PER : (k + 1) * PER, :].reshape(8 * PER, WIDE)
        result = nt(tokens, w3[...])
        proj_s[k] = result[:, 256:512].astype(BF)
        send(proj_s.at[k], proj_r.at[k], sib_s.at[0], sib_r.at[k], (sibling, col))
        keep_proj(result[:, 0:256], core, k)

    def from_sibling(k):
        arrive(proj_r.at[k], sib_r.at[k], sib_s.at[0])
        keep_proj(proj_r[k].astype(F32), 1 - core, k)

    weights_y(1)
    arrive(wt_other, wt_r.at[0], wt_s.at[0])
    w3[256:320, :] = (wt_other[0:64, :].astype(F32) * 0.125).astype(BF)
    w3[320:448, :] = wt_other[64:192, :]
    w3[448:512, :] = jnp.zeros((64, WIDE), BF)

    gather(0)
    relay(0)
    for k in range(1, CHUNKS):
        gather(k)
        finish(k - 1)
        relay(k)
        project(k - 1)
        if k > 1:
            from_sibling(k - 2)
    finish(CHUNKS - 1)
    project(CHUNKS - 1)
    from_sibling(CHUNKS - 2)
    from_sibling(CHUNKS - 1)

    low = iota((32, 128), 1) < 64
    keys = keys_all[...].reshape(WIDE, 128)
    values = values_all[...].reshape(WIDE, 128)

    turns = (2, 1, 3, 0)

    def score(turn):
        return nt(asked_all[:, ((xx + turns[turn]) & 3)].reshape(256, 128), keys)

    for sem in (xr_s.at[0], xl_s.at[0]):
        sent_by(sem, tok.at[:, 0, 0])
    for side in range(2):
        sent_by(xf_s.at[side], tok.at[side, 0, 0])
    sent_by(sib_s.at[0], proj_s)

    scores = score(0)
    for turn in range(4):
        following = score(turn + 1) if turn < 3 else None
        weights = jnp.exp(scores - jnp.max(scores, 1, keepdims=True)).astype(BF)
        mixed = mm(weights, values)
        mixed = mixed / pltpu.roll(mixed, 64, 1)
        for which in range(4):
            at = 64 * which
            packed = jnp.where(low, mixed[at : at + 32], pltpu.roll(mixed[at + 32 : at + 64], 64, 1))
            ret_s[turn, which // 2, which % 2] = packed.astype(BF)
        for side in range(2):
            target = side * 8 + ((xx + turns[turn]) & 3) * 2 + core
            send(ret_s.at[turn, side], ret_r.at[turn, half], back_s.at[0], back_r.at[turn], (target, far_col))
        scores = following

    load_up.wait()
    load_skip.wait()
    load_solver.wait()
    pixels = merged[...].astype(F32)
    table = solver_ref[...]
    table = jnp.where(iota(table.shape, 1) == step_ref[0], table, 0.0)
    keep = jnp.sum(table[0:1], 1, keepdims=True)
    gain = jnp.sum(table[1:2], 1, keepdims=True)
    skip = skip_ref[...].reshape(1, 256)
    base = keep * noisy_m[...].astype(F32) + gain * (jnp.concatenate([skip] * 4, 1) * pixels)
    i = iota((256, 256), 0)
    r, c = i >> 3, i & 7
    block = r >> 3
    spot = jnp.where((block == 1) | (block == 2), block - 1, jnp.where(block == third, 2, 3))
    source = (2 * (r & 1) + (c & 1)) * 64 + spot * 16 + ((r >> 1) & 3) * 4 + (c >> 1)
    unshuffle = (iota((256, 256), 1) == source).astype(F32).astype(BF)
    for far in range(2):
        arrive(wo.at[pl.ds(0, 4), pl.ds(0, 48)], w3_r.at[far], w3_s.at[far])
    for d in range(8):

        @pl.when(there[d])
        def _():
            halo_copy(d).wait_send()

    wait_sent()

    def head_rows(turn, which):
        even, odd = ret_r[turn, 0, which].astype(F32), ret_r[turn, 1, which].astype(F32)
        first = jnp.where(low, even, pltpu.roll(odd, 64, 1))
        second = jnp.where(low, pltpu.roll(even, 64, 1), odd)
        return jnp.concatenate([first, second], 0).astype(BF)

    shares = [None, None]
    for couple in range(2):
        weight = []
        for turn in (2 * couple, 2 * couple + 1):
            arrive(ret_r.at[turn], back_r.at[turn], back_s.at[0])
            from_x = (xx + 4 - turns[turn]) & 3
            weight += [wo[from_x], wo[4 + from_x]]
        weight = jnp.concatenate(weight, 0)
        for at, which in enumerate((1 - core, core)):
            heads = jnp.concatenate([head_rows(2 * couple, which), head_rows(2 * couple + 1, which)], 1)
            share = mm(heads, weight)
            shares[at] = share if couple == 0 else shares[at] + share
            if couple == 1 and at == 0:
                share_s[...] = shares[0].astype(BF)
                send(share_s, share_r, share_sems.at[0], share_sems.at[1], (sibling, col))
    coarse_next = pixels + shares[1]
    arrive(share_r, share_sems.at[1], share_sems.at[0])
    coarse_next = coarse_next + share_r[...].astype(F32)
    upsampled = mm(coarse_next.astype(BF), wup[...])
    sent_by(back_s.at[0], ret_s)
    sent_by(share_sems.at[0], share_s)
    wait_sent()
    result = base + gain * upsampled
    stacked = jnp.concatenate([result[:, ab * 256 : ab * 256 + 256] for ab in range(4)], 0)
    upper = stacked.astype(BF)
    lower = (stacked - upper.astype(F32)).astype(BF)
    out_ref[...] = (mm(unshuffle, upper) + mm(unshuffle, lower)).reshape(32, 8, 256)


def shards(
    noisy_image,
    time_index,
    solver_index,
    time_gains,
    pixel_qkv,
    pixel_out,
    coarse_gains,
    coarse_qkv,
    coarse_out,
    upsample_weight,
    skip_gain,
    solver_table,
):
    vmem = pl.BlockSpec(memory_space=pltpu.VMEM)
    smem = pl.BlockSpec(memory_space=pltpu.SMEM)
    hbm = pl.BlockSpec(memory_space=pltpu.HBM)
    dma = pltpu.SemaphoreType.DMA
    return pl.pallas_call(
        kernel,
        out_shape=jax.ShapeDtypeStruct((32, 8, 256), F32),
        in_specs=[smem] * 2 + [hbm] * 10,
        out_specs=vmem,
        scratch_shapes=[
            pltpu.VMEM((32, 8, 256), BF),
            pltpu.VMEM((2, 32), F32),
            pltpu.VMEM((32, 256), F32),
            pltpu.VMEM((256, 768), BF),
            pltpu.VMEM((256, 256), BF),
            pltpu.VMEM((32, WIDE), F32),
            pltpu.VMEM((256,), F32),
            pltpu.VMEM((320, 256), BF),
            pltpu.VMEM((160, 256), BF),
            pltpu.VMEM((160, 256), BF),
            pltpu.VMEM((128, 256), BF),
            pltpu.VMEM((128, 256), BF),
            pltpu.VMEM((320, 512), BF),
            pltpu.VMEM((320, 512), BF),
            pltpu.VMEM((256, 256), BF),
            pltpu.VMEM((64, WIDE), BF),
            pltpu.VMEM((64, WIDE), BF),
            pltpu.VMEM((64, WIDE), BF),
            pltpu.VMEM((2, 2, 2, 64, WIDE), BF),
            pltpu.VMEM((192, WIDE), BF),
            pltpu.VMEM((192, WIDE), BF),
            pltpu.VMEM((512, WIDE), BF),
            pltpu.VMEM((8, 64, WIDE), BF),
            pltpu.VMEM((WIDE, WIDE), BF),
            pltpu.VMEM((2, 4, 2, 64, 128), BF),
            pltpu.VMEM((2, 4, 2, 64, 128), BF),
            pltpu.VMEM((2, 4, 2, 64, 128), BF),
            pltpu.VMEM((CHUNKS, 8 * PER, 256), BF),
            pltpu.VMEM((CHUNKS, 8 * PER, 256), BF),
            pltpu.VMEM((4, 2, 2, 32, 128), BF),
            pltpu.VMEM((4, 2, 2, 32, 128), BF),
            pltpu.VMEM((64, WIDE), BF),
            pltpu.VMEM((64, WIDE), BF),
            dma((8,)),
            dma((8,)),
            dma((2,)),
            dma((CHUNKS,)),
            dma((1,)),
            dma((CHUNKS,)),
            dma((1,)),
            dma((CHUNKS,)),
            dma((2,)),
            dma((CHUNKS,)),
            dma((1,)),
            dma((CHUNKS,)),
            dma((1,)),
            dma((1,)),
            dma((2,)),
            dma((2,)),
            dma((2,)),
            dma((2,)),
            dma((1,)),
            dma((1,)),
            dma((2,)),
            dma((1,)),
            dma((4,)),
            dma((10,)),
        ],
        compiler_params=pltpu.CompilerParams(
            collective_id=0, has_side_effects=True, vmem_limit_bytes=48 * 1024 * 1024
        ),
        cost_estimate=pl.CostEstimate(flops=2_000_000_000, bytes_accessed=8_000_000, transcendentals=1_300_000),
    )(
        time_index,
        solver_index,
        *(
            pltpu.with_memory_space_constraint(array, pltpu.HBM)
            for array in (
                noisy_image,
                solver_table.T,
                time_gains,
                pixel_qkv,
                pixel_out,
                coarse_gains,
                skip_gain,
                coarse_qkv.reshape(coarse_qkv.shape[0], coarse_qkv.shape[2]).T,
                coarse_out,
                upsample_weight,
            )
        ),
    )


def solution(mesh):
    placed = (
        P("row", "col", None),
        P(),
        P(),
        P(),
        P(),
        P(),
        P(),
        P(None, "row", None),
        P("row", None),
        P(),
        P(),
        P(),
    )
    return jax.shard_map(
        shards, mesh=mesh, in_specs=placed, out_specs=P("row", "col", None), check_vma=False
    )
```

```python
import jax
import jax.numpy as jnp
from jax import lax
from jax.experimental import pallas as pl
from jax.experimental.pallas import tpu as pltpu
from jax.sharding import PartitionSpec as P

MESH = pl.DeviceIdType.MESH
BF = jnp.bfloat16
F32 = jnp.float32
ROWS, COLS = 16, 32
TOKENS = 64
WIDE = 1024
CHUNKS = 4
PER = TOKENS // CHUNKS
DIRS = ((-1, 0), (1, 0), (0, -1), (0, 1), (-1, -1), (-1, 1), (1, -1), (1, 1))


def iota(shape, dim):
    return lax.broadcasted_iota(jnp.int32, shape, dim)


def nt(left, right):
    return lax.dot_general(left, right, (((1,), (1,)), ((), ())), preferred_element_type=F32)


def mm(left, right):
    return jnp.dot(left, right, preferred_element_type=F32)


def norm(floats, scales):
    factor = lax.rsqrt(jnp.mean(floats * floats, -1, keepdims=True) + 1e-06)
    return (floats * factor * scales).astype(BF)


def pick(table, index):
    hit = iota(table.shape, 0) == index
    return jnp.sum(jnp.where(hit, table, 0.0), 0, keepdims=True)


def kernel(
    time_ref,
    step_ref,
    noisy_hbm,
    solver_hbm,
    gains_hbm,
    qkv_hbm,
    pout_hbm,
    cgains_hbm,
    skip_hbm,
    cqkv_hbm,
    cout_hbm,
    up_hbm,
    out_ref,
    noisy_ref,
    solver_ref,
    gains_ref,
    qkv_ref,
    pout_ref,
    cgains_ref,
    skip_ref,
    cc,
    ll,
    rr,
    pack_l,
    pack_r,
    relayed,
    kv_c,
    kv_e,
    query,
    noisy_m,
    merged,
    own,
    tok,
    wt,
    wt_other,
    w3,
    wo,
    wup,
    asked_all,
    keys_all,
    values_all,
    proj_s,
    proj_r,
    ret_s,
    ret_r,
    share_s,
    share_r,
    halo_s,
    halo_r,
    seam_s,
    seam_r,
    hand_s,
    z_s,
    z_r,
    xr_s,
    xr_r,
    xl_s,
    xl_r,
    xf_s,
    xf_r,
    sib_s,
    sib_r,
    w1_s,
    w1_r,
    w2_s,
    w2_r,
    w3_s,
    w3_r,
    wt_s,
    wt_r,
    share_sems,
    back_s,
    back_r,
    local,
):
    row, col = lax.axis_index("row"), lax.axis_index("col")
    half, xx, core = row >> 3, (row >> 1) & 3, row & 1
    yy = col & 3
    group = row >> 1
    far_col = (col + 16) & 31
    far_row = (row + 8) & 15
    sibling = row + 1 - 2 * core

    fourth = jnp.where(row == 8, 0, 3)
    third = 3 - fourth

    def x_row(shift):
        return half * 8 + ((xx + shift) & 3) * 2 + core

    def y_col(shift):
        return col - yy + ((yy + shift) & 3)

    def remote(src, dst, send, recv, where):
        return pltpu.make_async_remote_copy(
            src_ref=src, dst_ref=dst, send_sem=send, recv_sem=recv, device_id=where, device_id_type=MESH
        )

    def arrive(dst, recv, send):
        remote(dst, dst, send, recv, (row, col)).wait_recv()

    sent = []

    def send(*args):
        remote(*args).start()

    def sent_by(sem, ref):
        sent.append((sem, ref))

    def wait_sent():
        for sem, ref in sent:
            remote(ref, ref, sem, local.at[0], (row, col)).wait_send()
        sent.clear()

    def load(src, dst, at):
        copy = pltpu.make_async_copy(src, dst, local.at[at])
        copy.start()
        return copy

    load_noisy = load(noisy_hbm, noisy_ref, 3)

    barrier = pltpu.get_barrier_semaphore()

    def greet(where):
        pl.semaphore_signal(barrier, inc=1, device_id=where, device_id_type=MESH)

    there = []
    for down, right in DIRS:
        r, c = row + down, col + right
        inside = (r >= 0) & (r < ROWS) & (c >= 0) & (c < COLS)
        there.append(inside & (row != 7) if down == 1 else inside)

        @pl.when(inside & (row != 8) if down == -1 else inside)
        def _():
            greet((row + down, col + right))

    for right in (-1, 0, 1):

        @pl.when((row == 0) & (far_col + right >= 0) & (far_col + right < COLS))
        def _():
            greet((7, far_col + right))


    greet((row, far_col))
    greet((far_row, far_col))
    for shift in (1, 2, 3):
        greet((x_row(shift), col))
        greet((row, y_col(shift)))
    greet((sibling, col))
    partners = 2 + 6 + 1
    seam = [(row == 7) & (col + right >= 0) & (col + right < COLS) for right in (0, 1, -1)]
    for flag in there + seam:
        partners = partners + flag.astype(jnp.int32)

    quarter = pl.ds(pl.multiple_of(yy * 16, 16), 16)
    own_quarter = wo.at[group, quarter]
    load_wo = load(cout_hbm.at[quarter], own_quarter, 0)
    load_gains = load(gains_hbm, gains_ref, 4)
    load_qkv = load(qkv_hbm, qkv_ref, 5)

    load_noisy.wait()
    tile = noisy_ref[...].astype(F32).reshape(256, 256)
    tile_b = tile.astype(BF)
    cc[32:288, :] = tile_b
    spot = iota((128, 256), 0)
    place = (spot >> 2) * 8 + (spot & 3)
    lane = iota((128, 256), 1)
    pack_l[...] = mm((lane == place).astype(F32).astype(BF), tile_b).astype(BF)
    pack_r[...] = mm((lane == place + 4).astype(F32).astype(BF), tile_b).astype(BF)

    pl.semaphore_wait(barrier, partners)

    halo = (
        (cc.at[32:64], cc.at[288:320]),
        (cc.at[256:288], cc.at[0:32]),
        (pack_l, rr.at[16:144]),
        (pack_r, ll.at[16:144]),
        (pack_l.at[0:16], rr.at[144:160]),
        (pack_r.at[0:16], ll.at[144:160]),
        (pack_l.at[112:128], rr.at[0:16]),
        (pack_r.at[112:128], ll.at[0:16]),
    )

    def halo_copy(d):
        src, dst = halo[d]
        return remote(src, dst, halo_s.at[d], halo_r.at[d], (row + DIRS[d][0], col + DIRS[d][1]))

    for d in (2, 3, 0, 1, 4, 5, 6, 7):

        @pl.when(there[d])
        def _():
            halo_copy(d).start()

    slots = (relayed.at[0:32], relayed.at[32:48], relayed.at[48:64])

    def seam_copy(piece):
        src = (cc.at[256:288], pack_r.at[112:128], pack_l.at[112:128])[piece]
        c = col + (0, 1, -1)[piece]
        where = (0, (c + 16) & 31)
        return remote(src, slots[piece], seam_s.at[piece], seam_r.at[piece], where)

    def hand_copy(piece):
        d = (1, 7, 6)[piece]
        return remote(slots[piece], halo[d][1], hand_s.at[piece], halo_r.at[d], (8, far_col))

    handed = [(row == 0) & (far_col + right >= 0) & (far_col + right < COLS) for right in (0, -1, 1)]
    for piece in range(3):

        @pl.when(seam[piece])
        def _():
            seam_copy(piece).start()

    from_there = []
    for down, right in DIRS:
        r, c = row - down, col - right
        from_there.append((r >= 0) & (r < ROWS) & (c >= 0) & (c < COLS))
    for d in range(8):

        @pl.when(jnp.logical_not(from_there[d]))
        def _():
            dst = halo[d][1]
            dst[...] = jnp.zeros(dst.shape, BF)

    load_pout = load(pout_hbm, pout_ref, 6)
    load_cgains = load(cgains_hbm, cgains_ref, 7)
    load_wt = load(cqkv_hbm, wt, 1)
    load_skip = load(skip_hbm, skip_ref, 8)
    load_solver = load(solver_hbm, solver_ref, 9)
    load_up = load(up_hbm, wup, 2)

    load_wo.wait()
    send(own_quarter, own_quarter, w1_s.at[0], w1_r.at[0], (far_row, far_col))
    sent_by(w1_s.at[0], own_quarter)
    three = pl.ds(0, 3)
    for shift in (1, 2, 3):
        send(own_quarter, own_quarter, w2_s.at[0], w2_r.at[0], (x_row(shift), col))

    load_gains.wait()
    scales = pick(gains_ref[...], time_ref[0])
    normed = norm(tile, scales)
    load_qkv.wait()
    kv_c[32:288, :] = mm(normed, qkv_ref[:, 256:768]).astype(BF)
    i = iota((256, 256), 0)
    spot, a, b, p, q = i >> 6, (i >> 5) & 1, (i >> 4) & 1, (i >> 2) & 3, i & 3
    blk = jnp.where(spot < 2, spot + 1, jnp.where(spot == 2, third, fourth))
    source = (8 * blk + 2 * p + a) * 8 + 2 * q + b
    shuffle = (iota((256, 256), 1) == source).astype(F32).astype(BF)
    noisy_q = mm(shuffle, tile_b)
    normed_q = mm(shuffle, normed).astype(BF)
    query[...] = mm(normed_q, qkv_ref[:, 0:256]).astype(BF)
    noisy_qb = noisy_q.astype(BF)
    for block in range(4):
        for ab in range(4):
            at = block * 64 + ab * 16
            noisy_m[block * 16 : block * 16 + 16, ab * 256 : ab * 256 + 256] = noisy_qb[at : at + 16]

    load_wt.wait()
    send(wt, wt_other, wt_s.at[0], wt_r.at[0], (sibling, col))
    sent_by(wt_s.at[0], wt)
    w3[0:64, :] = (wt[0:64, :].astype(F32) * 0.125).astype(BF)
    w3[64:192, :] = wt[64:192, :]
    w3[192:256, :] = jnp.zeros((64, WIDE), BF)

    def halo_wait(d, flag):
        @pl.when(from_there[d] & flag)
        def _():
            arrive(halo[d][1], halo_r.at[d], halo_s.at[d])

    def edge_kv(array):
        return mm(norm(array.astype(F32), scales), qkv_ref[:, 256:768]).astype(BF)

    for piece in range(3):

        @pl.when(handed[piece])
        def _():
            arrive(slots[piece], seam_r.at[piece], seam_s.at[piece])
            hand_copy(piece).start()

    halo_wait(2, True)
    halo_wait(3, True)
    sides = edge_kv(jnp.concatenate([ll[16:144, :], rr[16:144, :]], 0))
    kv_e[16:144, :] = sides[0:128]
    kv_e[176:304, :] = sides[128:256]

    def outer_edge(block, last):
        above = (row == 8) if last else (row != 8)
        for d in (1, 6, 7):
            halo_wait(d, above)
        for d in (0, 4, 5):
            halo_wait(d, jnp.logical_not(above))
        wide = pl.ds(pl.multiple_of(jnp.where(block == 0, 0, 288), 32), 32)
        start = jnp.where(block == 0, 0, 144)
        narrow = pl.ds(pl.multiple_of(start, 16), 16)
        result = edge_kv(jnp.concatenate([cc[wide, :], ll[narrow, :], rr[narrow, :]], 0))
        kv_c[wide, :] = result[0:32]
        kv_e[narrow, :] = result[32:48]
        kv_e[pl.ds(pl.multiple_of(160 + start, 16), 16), :] = result[48:64]

    j = iota((64, 256), 1)
    in_c = j < 128
    key_row = jnp.where(in_c, j >> 3, (j & 63) >> 2) - 4
    key_col = jnp.where(in_c, j & 7, (j & 3) + jnp.where(j < 192, -4, 8))
    i = iota((64, 256), 0)
    query_row = 2 * ((i >> 2) & 3) + ((i >> 5) & 1)
    query_col = 2 * (i & 3) + ((i >> 4) & 1)
    full_col = key_col + col * 8
    near = (
        (jnp.abs(key_row - query_row) <= 3)
        & (jnp.abs(key_col - query_col) <= 3)
        & (full_col >= 0)
        & (full_col < 256)
    )
    head_of = iota((64, 256), 1) >> 6
    ones = jnp.ones((256, 256), BF)
    load_cgains.wait()
    load_pout.wait()
    coarse_scales = pick(cgains_ref[...], time_ref[0])

    def window_block(spot, block):
        inner = pl.ds(pl.multiple_of(64 * block, 64), 128)
        lefts = pl.ds(pl.multiple_of(32 * block, 32), 64)
        rights = pl.ds(pl.multiple_of(160 + 32 * block, 32), 64)
        keys = jnp.concatenate([kv_c[inner, 0:256], kv_e[lefts, 0:256], kv_e[rights, 0:256]], 0)
        values = jnp.concatenate([kv_c[inner, 256:512], kv_e[lefts, 256:512], kv_e[rights, 256:512]], 0)
        asked = query[64 * spot : 64 * spot + 64, :].astype(F32) * 0.125
        spread = jnp.concatenate([jnp.where(head_of == h, asked, 0.0) for h in range(4)], 0).astype(BF)
        full_row = key_row + (row * 32 + 8 * block)
        usable = near & (full_row >= 0) & (full_row < 512)
        bias = jnp.where(usable, 0.0, -1e30)
        scores = nt(spread, keys) + jnp.concatenate([bias] * 4, 0)
        weights = jnp.exp(scores - jnp.max(scores, 1, keepdims=True)).astype(BF)
        sums = mm(weights, ones)
        mixed = mm(weights, values)
        total, share = jnp.zeros((64, 256), F32), jnp.zeros((64, 256), F32)
        for h in range(4):
            total = jnp.where(head_of == h, sums[64 * h : 64 * h + 64], total)
            share = jnp.where(head_of == h, mixed[64 * h : 64 * h + 64], share)
        attended = (share / total).astype(BF)
        delta = mm(attended, pout_ref[...])
        for ab in range(4):
            rows, lanes = pl.ds(spot * 16, 16), pl.ds(ab * 256, 256)
            pixels = noisy_m[rows, lanes].astype(F32) + delta[ab * 16 : ab * 16 + 16]
            merged[rows, lanes] = pixels.astype(BF)

    def part(k):
        return pl.ds(k * PER, PER)

    def weights_x():
        ref = wo.at[far_row >> 1, quarter]
        arrive(ref, w1_r.at[0], w1_s.at[0])
        for shift in (1, 2, 3):
            send(ref, ref, w2_s.at[1], w2_r.at[1], (x_row(shift), col))

    def weights_y(far):
        arrive(wo.at[three, quarter], w2_r.at[far], w2_s.at[far])
        sent_by(w2_s.at[far], wo.at[three, quarter])
        side = 1 - half if far else half
        ref = wo.at[pl.ds(pl.multiple_of(side * 4, 4), 4), quarter]
        for shift in (1, 2, 3):
            send(ref, ref, w3_s.at[far], w3_r.at[far], (row, y_col(shift)))
        sent_by(w3_s.at[far], wo.at[pl.ds(0, 4), pl.ds(0, 48)])

    for k in range(CHUNKS):
        if k == 1:
            weights_y(0)
        if k == 2:
            weights_x()
        if k == 3:
            weights_y(1)
        if k < 2:
            window_block(k, k + 1)
        else:
            outer_edge(third if k == 2 else fourth, k == 3)
            window_block(k, third if k == 2 else fourth)
        own[part(k), :] = norm(merged[part(k), :].astype(F32), coarse_scales)
        for t, target in enumerate((row, far_row)):
            send(
                own.at[part(k)],
                tok.at[half, xx >> 1, xx & 1, part(k)],
                z_s.at[t],
                z_r.at[k],
                (target, far_col),
            )
    for t in range(2):
        sent_by(z_s.at[t], own)

    def blocks(shift, k):
        at = (xx + shift) & 3
        return tok.at[:, at >> 1, at & 1, part(k)]

    def one(side, shift, k):
        at = (xx + shift) & 3
        return tok.at[side, at >> 1, at & 1, part(k)]

    def gather(k):
        ref = blocks(0, k)
        arrive(ref, z_r.at[k], z_s.at[0])
        send(ref, ref, xr_s.at[0], xr_r.at[k], (x_row(1), col))
        send(ref, ref, xl_s.at[0], xl_r.at[k], (x_row(3), col))

    def relay(k):
        arrive(blocks(3, k), xr_r.at[k], xr_s.at[0])
        ref = one(0, 3, k)
        send(ref, ref, xf_s.at[0], xf_r.at[k], (x_row(1), col))
        arrive(blocks(1, k), xl_r.at[k], xl_s.at[0])
        ref = one(1, 1, k)
        send(ref, ref, xf_s.at[1], xf_r.at[k], (x_row(3), col))

    def finish(k):
        arrive(blocks(2, k), xf_r.at[k], xf_s.at[0])

    left = iota((8 * PER, 128), 1) < 64

    def keep_proj(result, which, k):
        both, value = result[:, 0:128], result[:, 128:256]
        for ref, array in (
            (asked_all, jnp.where(left, both, 0.0)),
            (keys_all, pltpu.roll(both, 64, 1)),
            (values_all, jnp.where(left, value, 1.0)),
        ):
            ref[:, :, which, k * PER : (k + 1) * PER, :] = array.astype(BF).reshape(2, 4, PER, 128)

    def project(k):
        tokens = tok[:, :, :, k * PER : (k + 1) * PER, :].reshape(8 * PER, WIDE)
        result = nt(tokens, w3[...])
        proj_s[k] = result[:, 256:512].astype(BF)
        send(proj_s.at[k], proj_r.at[k], sib_s.at[0], sib_r.at[k], (sibling, col))
        keep_proj(result[:, 0:256], core, k)

    def from_sibling(k):
        arrive(proj_r.at[k], sib_r.at[k], sib_s.at[0])
        keep_proj(proj_r[k].astype(F32), 1 - core, k)

    arrive(wt_other, wt_r.at[0], wt_s.at[0])
    w3[256:320, :] = (wt_other[0:64, :].astype(F32) * 0.125).astype(BF)
    w3[320:448, :] = wt_other[64:192, :]
    w3[448:512, :] = jnp.zeros((64, WIDE), BF)

    gather(0)
    relay(0)
    for k in range(1, CHUNKS):
        gather(k)
        finish(k - 1)
        relay(k)
        project(k - 1)
        if k > 1:
            from_sibling(k - 2)
    finish(CHUNKS - 1)
    project(CHUNKS - 1)
    from_sibling(CHUNKS - 2)
    from_sibling(CHUNKS - 1)

    low = iota((32, 128), 1) < 64
    keys = keys_all[...].reshape(WIDE, 128)
    values = values_all[...].reshape(WIDE, 128)

    turns = (2, 1, 3, 0)

    def score(turn):
        return nt(asked_all[:, ((xx + turns[turn]) & 3)].reshape(256, 128), keys)

    for sem in (xr_s.at[0], xl_s.at[0]):
        sent_by(sem, tok.at[:, 0, 0])
    for side in range(2):
        sent_by(xf_s.at[side], tok.at[side, 0, 0])
    sent_by(sib_s.at[0], proj_s)

    scores = score(0)
    for turn in range(4):
        following = score(turn + 1) if turn < 3 else None
        weights = jnp.exp(scores - jnp.max(scores, 1, keepdims=True)).astype(BF)
        mixed = mm(weights, values)
        mixed = mixed / pltpu.roll(mixed, 64, 1)
        for which in range(4):
            at = 64 * which
            packed = jnp.where(low, mixed[at : at + 32], pltpu.roll(mixed[at + 32 : at + 64], 64, 1))
            ret_s[turn, which // 2, which % 2] = packed.astype(BF)
        for side in range(2):
            target = side * 8 + ((xx + turns[turn]) & 3) * 2 + core
            send(ret_s.at[turn, side], ret_r.at[turn, half], back_s.at[0], back_r.at[turn], (target, far_col))
        scores = following

    load_up.wait()
    load_skip.wait()
    load_solver.wait()
    pixels = merged[...].astype(F32)
    table = solver_ref[...]
    table = jnp.where(iota(table.shape, 1) == step_ref[0], table, 0.0)
    keep = jnp.sum(table[0:1], 1, keepdims=True)
    gain = jnp.sum(table[1:2], 1, keepdims=True)
    skip = skip_ref[...].reshape(1, 256)
    base = keep * noisy_m[...].astype(F32) + gain * (jnp.concatenate([skip] * 4, 1) * pixels)
    i = iota((256, 256), 0)
    r, c = i >> 3, i & 7
    block = r >> 3
    spot = jnp.where((block == 1) | (block == 2), block - 1, jnp.where(block == third, 2, 3))
    source = (2 * (r & 1) + (c & 1)) * 64 + spot * 16 + ((r >> 1) & 3) * 4 + (c >> 1)
    unshuffle = (iota((256, 256), 1) == source).astype(F32).astype(BF)
    for far in range(2):
        arrive(wo.at[pl.ds(0, 4), pl.ds(0, 48)], w3_r.at[far], w3_s.at[far])
    for d in range(8):

        @pl.when(there[d])
        def _():
            halo_copy(d).wait_send()

    for piece in range(3):

        @pl.when(seam[piece])
        def _():
            seam_copy(piece).wait_send()

        @pl.when(handed[piece])
        def _():
            hand_copy(piece).wait_send()

    wait_sent()

    def head_rows(turn, which):
        even, odd = ret_r[turn, 0, which].astype(F32), ret_r[turn, 1, which].astype(F32)
        first = jnp.where(low, even, pltpu.roll(odd, 64, 1))
        second = jnp.where(low, pltpu.roll(even, 64, 1), odd)
        return jnp.concatenate([first, second], 0).astype(BF)

    shares = [None, None]
    for couple in range(2):
        weight = []
        for turn in (2 * couple, 2 * couple + 1):
            arrive(ret_r.at[turn], back_r.at[turn], back_s.at[0])
            from_x = (xx + 4 - turns[turn]) & 3
            weight += [wo[from_x], wo[4 + from_x]]
        weight = jnp.concatenate(weight, 0)
        for at, which in enumerate((1 - core, core)):
            heads = jnp.concatenate([head_rows(2 * couple, which), head_rows(2 * couple + 1, which)], 1)
            share = mm(heads, weight)
            shares[at] = share if couple == 0 else shares[at] + share
            if couple == 1 and at == 0:
                share_s[...] = shares[0].astype(BF)
                send(share_s, share_r, share_sems.at[0], share_sems.at[1], (sibling, col))
    coarse_next = pixels + shares[1]
    arrive(share_r, share_sems.at[1], share_sems.at[0])
    coarse_next = coarse_next + share_r[...].astype(F32)
    upsampled = mm(coarse_next.astype(BF), wup[...])
    sent_by(back_s.at[0], ret_s)
    sent_by(share_sems.at[0], share_s)
    wait_sent()
    result = base + gain * upsampled
    stacked = jnp.concatenate([result[:, ab * 256 : ab * 256 + 256] for ab in range(4)], 0)
    upper = stacked.astype(BF)
    lower = (stacked - upper.astype(F32)).astype(BF)
    out_ref[...] = (mm(unshuffle, upper) + mm(unshuffle, lower)).reshape(32, 8, 256)


def shards(
    noisy_image,
    time_index,
    solver_index,
    time_gains,
    pixel_qkv,
    pixel_out,
    coarse_gains,
    coarse_qkv,
    coarse_out,
    upsample_weight,
    skip_gain,
    solver_table,
):
    vmem = pl.BlockSpec(memory_space=pltpu.VMEM)
    smem = pl.BlockSpec(memory_space=pltpu.SMEM)
    hbm = pl.BlockSpec(memory_space=pltpu.HBM)
    dma = pltpu.SemaphoreType.DMA
    return pl.pallas_call(
        kernel,
        out_shape=jax.ShapeDtypeStruct((32, 8, 256), F32),
        in_specs=[smem] * 2 + [hbm] * 10,
        out_specs=vmem,
        scratch_shapes=[
            pltpu.VMEM((32, 8, 256), BF),
            pltpu.VMEM((2, 32), F32),
            pltpu.VMEM((32, 256), F32),
            pltpu.VMEM((256, 768), BF),
            pltpu.VMEM((256, 256), BF),
            pltpu.VMEM((32, WIDE), F32),
            pltpu.VMEM((256,), F32),
            pltpu.VMEM((320, 256), BF),
            pltpu.VMEM((160, 256), BF),
            pltpu.VMEM((160, 256), BF),
            pltpu.VMEM((128, 256), BF),
            pltpu.VMEM((128, 256), BF),
            pltpu.VMEM((64, 256), BF),
            pltpu.VMEM((320, 512), BF),
            pltpu.VMEM((320, 512), BF),
            pltpu.VMEM((256, 256), BF),
            pltpu.VMEM((64, WIDE), BF),
            pltpu.VMEM((64, WIDE), BF),
            pltpu.VMEM((64, WIDE), BF),
            pltpu.VMEM((2, 2, 2, 64, WIDE), BF),
            pltpu.VMEM((192, WIDE), BF),
            pltpu.VMEM((192, WIDE), BF),
            pltpu.VMEM((512, WIDE), BF),
            pltpu.VMEM((8, 64, WIDE), BF),
            pltpu.VMEM((WIDE, WIDE), BF),
            pltpu.VMEM((2, 4, 2, 64, 128), BF),
            pltpu.VMEM((2, 4, 2, 64, 128), BF),
            pltpu.VMEM((2, 4, 2, 64, 128), BF),
            pltpu.VMEM((CHUNKS, 8 * PER, 256), BF),
            pltpu.VMEM((CHUNKS, 8 * PER, 256), BF),
            pltpu.VMEM((4, 2, 2, 32, 128), BF),
            pltpu.VMEM((4, 2, 2, 32, 128), BF),
            pltpu.VMEM((64, WIDE), BF),
            pltpu.VMEM((64, WIDE), BF),
            dma((8,)),
            dma((8,)),
            dma((3,)),
            dma((3,)),
            dma((3,)),
            dma((2,)),
            dma((CHUNKS,)),
            dma((1,)),
            dma((CHUNKS,)),
            dma((1,)),
            dma((CHUNKS,)),
            dma((2,)),
            dma((CHUNKS,)),
            dma((1,)),
            dma((CHUNKS,)),
            dma((1,)),
            dma((1,)),
            dma((2,)),
            dma((2,)),
            dma((2,)),
            dma((2,)),
            dma((1,)),
            dma((1,)),
            dma((2,)),
            dma((1,)),
            dma((4,)),
            dma((10,)),
        ],
        compiler_params=pltpu.CompilerParams(
            collective_id=0, has_side_effects=True, vmem_limit_bytes=48 * 1024 * 1024
        ),
        cost_estimate=pl.CostEstimate(flops=2_000_000_000, bytes_accessed=8_000_000, transcendentals=1_300_000),
    )(
        time_index,
        solver_index,
        *(
            pltpu.with_memory_space_constraint(array, pltpu.HBM)
            for array in (
                noisy_image,
                solver_table.T,
                time_gains,
                pixel_qkv,
                pixel_out,
                coarse_gains,
                skip_gain,
                coarse_qkv.reshape(coarse_qkv.shape[0], coarse_qkv.shape[2]).T,
                coarse_out,
                upsample_weight,
            )
        ),
    )


def solution(mesh):
    placed = (
        P("row", "col", None),
        P(),
        P(),
        P(),
        P(),
        P(),
        P(),
        P(None, "row", None),
        P("row", None),
        P(),
        P(),
        P(),
    )
    return jax.shard_map(
        shards, mesh=mesh, in_specs=placed, out_specs=P("row", "col", None), check_vma=False
    )
```

```python
import jax
import jax.numpy as jnp
from jax import lax
from jax.experimental import pallas as pl
from jax.experimental.pallas import tpu as pltpu
from jax.sharding import PartitionSpec as P

MESH = pl.DeviceIdType.MESH
BF = jnp.bfloat16
F32 = jnp.float32
ROWS, COLS = 16, 32
TOKENS = 64
WIDE = 1024
CHUNKS = 4
PER = TOKENS // CHUNKS
DIRS = ((-1, 0), (1, 0), (0, -1), (0, 1), (-1, -1), (-1, 1), (1, -1), (1, 1))


def iota(shape, dim):
    return lax.broadcasted_iota(jnp.int32, shape, dim)


def nt(left, right):
    return lax.dot_general(left, right, (((1,), (1,)), ((), ())), preferred_element_type=F32)


def mm(left, right):
    return jnp.dot(left, right, preferred_element_type=F32)


def norm(floats, scales):
    factor = lax.rsqrt(jnp.mean(floats * floats, -1, keepdims=True) + 1e-06)
    return (floats * factor * scales).astype(BF)


def pick(table, index):
    hit = iota(table.shape, 0) == index
    return jnp.sum(jnp.where(hit, table, 0.0), 0, keepdims=True)


def kernel(
    time_ref,
    step_ref,
    noisy_hbm,
    solver_hbm,
    gains_hbm,
    qkv_hbm,
    pout_hbm,
    cgains_hbm,
    skip_hbm,
    cqkv_hbm,
    cout_hbm,
    up_hbm,
    out_ref,
    noisy_ref,
    solver_ref,
    gains_ref,
    qkv_ref,
    pout_ref,
    cgains_ref,
    skip_ref,
    cc,
    ll,
    rr,
    pack_l,
    pack_r,
    relayed,
    kv_c,
    kv_e,
    query,
    noisy_m,
    merged,
    own,
    tok,
    wt,
    wt_other,
    w3,
    wo,
    wup,
    asked_all,
    keys_all,
    values_all,
    proj_s,
    proj_r,
    ret_s,
    ret_r,
    share_s,
    share_r,
    halo_s,
    halo_r,
    seam_s,
    seam_r,
    hand_s,
    z_s,
    z_r,
    xr_s,
    xr_r,
    xl_s,
    xl_r,
    xf_s,
    xf_r,
    sib_s,
    sib_r,
    w1_s,
    w1_r,
    w2_s,
    w2_r,
    w3_s,
    w3_r,
    wt_s,
    wt_r,
    share_sems,
    back_s,
    back_r,
    local,
):
    row, col = lax.axis_index("row"), lax.axis_index("col")
    half, xx, core = row >> 3, (row >> 1) & 3, row & 1
    yy = col & 3
    group = row >> 1
    far_col = (col + 16) & 31
    far_row = (row + 8) & 15
    sibling = row + 1 - 2 * core

    fourth = jnp.where(row == 8, 0, 3)
    third = 3 - fourth

    def x_row(shift):
        return half * 8 + ((xx + shift) & 3) * 2 + core

    def y_col(shift):
        return col - yy + ((yy + shift) & 3)

    def remote(src, dst, send, recv, where):
        return pltpu.make_async_remote_copy(
            src_ref=src, dst_ref=dst, send_sem=send, recv_sem=recv, device_id=where, device_id_type=MESH
        )

    def arrive(dst, recv, send):
        remote(dst, dst, send, recv, (row, col)).wait_recv()

    sent = []

    def send(*args):
        remote(*args).start()

    def sent_by(sem, ref):
        sent.append((sem, ref))

    def wait_sent():
        for sem, ref in sent:
            remote(ref, ref, sem, local.at[0], (row, col)).wait_send()
        sent.clear()

    def load(src, dst, at):
        copy = pltpu.make_async_copy(src, dst, local.at[at])
        copy.start()
        return copy

    load_noisy = load(noisy_hbm, noisy_ref, 3)

    barrier = pltpu.get_barrier_semaphore()

    def greet(where):
        pl.semaphore_signal(barrier, inc=1, device_id=where, device_id_type=MESH)

    greet((row, far_col))
    greet((far_row, far_col))
    for right in (-1, 0, 1):

        @pl.when((row == 0) & (far_col + right >= 0) & (far_col + right < COLS))
        def _():
            greet((7, far_col + right))

    there = []
    for down, right in DIRS:
        r, c = row + down, col + right
        inside = (r >= 0) & (r < ROWS) & (c >= 0) & (c < COLS)
        there.append(inside & (row != 7) if down == 1 else inside)

        @pl.when(inside & (row != 8) if down == -1 else inside)
        def _():
            greet((row + down, col + right))

    for shift in (1, 2, 3):
        greet((x_row(shift), col))
        greet((row, y_col(shift)))
    greet((sibling, col))
    partners = 2 + 6 + 1
    seam = [(row == 7) & (col + right >= 0) & (col + right < COLS) for right in (0, 1, -1)]
    for flag in there + seam:
        partners = partners + flag.astype(jnp.int32)

    quarter = pl.ds(pl.multiple_of(yy * 16, 16), 16)
    own_quarter = wo.at[group, quarter]
    load_wo = load(cout_hbm.at[quarter], own_quarter, 0)
    load_gains = load(gains_hbm, gains_ref, 4)
    load_qkv = load(qkv_hbm, qkv_ref, 5)

    load_noisy.wait()
    tile = noisy_ref[...].astype(F32).reshape(256, 256)
    tile_b = tile.astype(BF)
    cc[32:288, :] = tile_b
    spot = iota((128, 256), 0)
    place = (spot >> 2) * 8 + (spot & 3)
    lane = iota((128, 256), 1)
    pack_l[...] = mm((lane == place).astype(F32).astype(BF), tile_b).astype(BF)
    pack_r[...] = mm((lane == place + 4).astype(F32).astype(BF), tile_b).astype(BF)

    pl.semaphore_wait(barrier, partners)

    halo = (
        (cc.at[32:64], cc.at[288:320]),
        (cc.at[256:288], cc.at[0:32]),
        (pack_l, rr.at[16:144]),
        (pack_r, ll.at[16:144]),
        (pack_l.at[0:16], rr.at[144:160]),
        (pack_r.at[0:16], ll.at[144:160]),
        (pack_l.at[112:128], rr.at[0:16]),
        (pack_r.at[112:128], ll.at[0:16]),
    )

    def halo_copy(d):
        src, dst = halo[d]
        return remote(src, dst, halo_s.at[d], halo_r.at[d], (row + DIRS[d][0], col + DIRS[d][1]))

    for d in (2, 3, 0, 1, 4, 5, 6, 7):

        @pl.when(there[d])
        def _():
            halo_copy(d).start()

    slots = (relayed.at[0:32], relayed.at[32:48], relayed.at[48:64])

    def seam_copy(piece):
        src = (cc.at[256:288], pack_r.at[112:128], pack_l.at[112:128])[piece]
        c = col + (0, 1, -1)[piece]
        where = (0, (c + 16) & 31)
        return remote(src, slots[piece], seam_s.at[piece], seam_r.at[piece], where)

    def hand_copy(piece):
        d = (1, 7, 6)[piece]
        return remote(slots[piece], halo[d][1], hand_s.at[piece], halo_r.at[d], (8, far_col))

    handed = [(row == 0) & (far_col + right >= 0) & (far_col + right < COLS) for right in (0, -1, 1)]
    for piece in range(3):

        @pl.when(seam[piece])
        def _():
            seam_copy(piece).start()

    from_there = []
    for down, right in DIRS:
        r, c = row - down, col - right
        from_there.append((r >= 0) & (r < ROWS) & (c >= 0) & (c < COLS))
    for d in range(8):

        @pl.when(jnp.logical_not(from_there[d]))
        def _():
            dst = halo[d][1]
            dst[...] = jnp.zeros(dst.shape, BF)

    load_pout = load(pout_hbm, pout_ref, 6)
    load_cgains = load(cgains_hbm, cgains_ref, 7)
    load_wt = load(cqkv_hbm, wt, 1)
    load_skip = load(skip_hbm, skip_ref, 8)
    load_solver = load(solver_hbm, solver_ref, 9)
    load_up = load(up_hbm, wup, 2)

    load_wo.wait()
    send(own_quarter, own_quarter, w1_s.at[0], w1_r.at[0], (far_row, far_col))
    sent_by(w1_s.at[0], own_quarter)
    three = pl.ds(0, 3)
    for shift in (1, 2, 3):
        send(own_quarter, own_quarter, w2_s.at[0], w2_r.at[0], (x_row(shift), col))

    load_gains.wait()
    scales = pick(gains_ref[...], time_ref[0])
    normed = norm(tile, scales)
    load_qkv.wait()
    kv_c[32:288, :] = mm(normed, qkv_ref[:, 256:768]).astype(BF)
    i = iota((256, 256), 0)
    spot, a, b, p, q = i >> 6, (i >> 5) & 1, (i >> 4) & 1, (i >> 2) & 3, i & 3
    blk = jnp.where(spot < 2, spot + 1, jnp.where(spot == 2, third, fourth))
    source = (8 * blk + 2 * p + a) * 8 + 2 * q + b
    shuffle = (iota((256, 256), 1) == source).astype(F32).astype(BF)
    noisy_q = mm(shuffle, tile_b)
    normed_q = mm(shuffle, normed).astype(BF)
    query[...] = mm(normed_q, qkv_ref[:, 0:256]).astype(BF)
    noisy_qb = noisy_q.astype(BF)
    for block in range(4):
        for ab in range(4):
            at = block * 64 + ab * 16
            noisy_m[block * 16 : block * 16 + 16, ab * 256 : ab * 256 + 256] = noisy_qb[at : at + 16]

    load_wt.wait()
    send(wt, wt_other, wt_s.at[0], wt_r.at[0], (sibling, col))
    sent_by(wt_s.at[0], wt)
    w3[0:64, :] = (wt[0:64, :].astype(F32) * 0.125).astype(BF)
    w3[64:192, :] = wt[64:192, :]
    w3[192:256, :] = jnp.zeros((64, WIDE), BF)

    def halo_wait(d, flag):
        @pl.when(from_there[d] & flag)
        def _():
            arrive(halo[d][1], halo_r.at[d], halo_s.at[d])

    def edge_kv(array):
        return mm(norm(array.astype(F32), scales), qkv_ref[:, 256:768]).astype(BF)

    for piece in range(3):

        @pl.when(handed[piece])
        def _():
            arrive(slots[piece], seam_r.at[piece], seam_s.at[piece])
            hand_copy(piece).start()

    halo_wait(2, True)
    halo_wait(3, True)
    sides = edge_kv(jnp.concatenate([ll[16:144, :], rr[16:144, :]], 0))
    kv_e[16:144, :] = sides[0:128]
    kv_e[176:304, :] = sides[128:256]

    def outer_edge(block, last):
        above = (row == 8) if last else (row != 8)
        for d in (1, 6, 7):
            halo_wait(d, above)
        for d in (0, 4, 5):
            halo_wait(d, jnp.logical_not(above))
        wide = pl.ds(pl.multiple_of(jnp.where(block == 0, 0, 288), 32), 32)
        start = jnp.where(block == 0, 0, 144)
        narrow = pl.ds(pl.multiple_of(start, 16), 16)
        result = edge_kv(jnp.concatenate([cc[wide, :], ll[narrow, :], rr[narrow, :]], 0))
        kv_c[wide, :] = result[0:32]
        kv_e[narrow, :] = result[32:48]
        kv_e[pl.ds(pl.multiple_of(160 + start, 16), 16), :] = result[48:64]

    j = iota((64, 256), 1)
    in_c = j < 128
    key_row = jnp.where(in_c, j >> 3, (j & 63) >> 2) - 4
    key_col = jnp.where(in_c, j & 7, (j & 3) + jnp.where(j < 192, -4, 8))
    i = iota((64, 256), 0)
    query_row = 2 * ((i >> 2) & 3) + ((i >> 5) & 1)
    query_col = 2 * (i & 3) + ((i >> 4) & 1)
    full_col = key_col + col * 8
    near = (
        (jnp.abs(key_row - query_row) <= 3)
        & (jnp.abs(key_col - query_col) <= 3)
        & (full_col >= 0)
        & (full_col < 256)
    )
    head_of = iota((64, 256), 1) >> 6
    ones = jnp.ones((256, 256), BF)
    load_cgains.wait()
    load_pout.wait()
    coarse_scales = pick(cgains_ref[...], time_ref[0])

    def window_block(spot, block):
        inner = pl.ds(pl.multiple_of(64 * block, 64), 128)
        lefts = pl.ds(pl.multiple_of(32 * block, 32), 64)
        rights = pl.ds(pl.multiple_of(160 + 32 * block, 32), 64)
        keys = jnp.concatenate([kv_c[inner, 0:256], kv_e[lefts, 0:256], kv_e[rights, 0:256]], 0)
        values = jnp.concatenate([kv_c[inner, 256:512], kv_e[lefts, 256:512], kv_e[rights, 256:512]], 0)
        asked = query[64 * spot : 64 * spot + 64, :].astype(F32) * 0.125
        spread = jnp.concatenate([jnp.where(head_of == h, asked, 0.0) for h in range(4)], 0).astype(BF)
        full_row = key_row + (row * 32 + 8 * block)
        usable = near & (full_row >= 0) & (full_row < 512)
        bias = jnp.where(usable, 0.0, -1e30)
        scores = nt(spread, keys) + jnp.concatenate([bias] * 4, 0)
        weights = jnp.exp(scores - jnp.max(scores, 1, keepdims=True)).astype(BF)
        sums = mm(weights, ones)
        mixed = mm(weights, values)
        total, share = jnp.zeros((64, 256), F32), jnp.zeros((64, 256), F32)
        for h in range(4):
            total = jnp.where(head_of == h, sums[64 * h : 64 * h + 64], total)
            share = jnp.where(head_of == h, mixed[64 * h : 64 * h + 64], share)
        attended = (share / total).astype(BF)
        delta = mm(attended, pout_ref[...])
        for ab in range(4):
            rows, lanes = pl.ds(spot * 16, 16), pl.ds(ab * 256, 256)
            pixels = noisy_m[rows, lanes].astype(F32) + delta[ab * 16 : ab * 16 + 16]
            merged[rows, lanes] = pixels.astype(BF)

    def part(k):
        return pl.ds(k * PER, PER)

    def weights_x():
        ref = wo.at[far_row >> 1, quarter]
        arrive(ref, w1_r.at[0], w1_s.at[0])
        for shift in (1, 2, 3):
            send(ref, ref, w2_s.at[1], w2_r.at[1], (x_row(shift), col))

    def weights_y(far):
        arrive(wo.at[three, quarter], w2_r.at[far], w2_s.at[far])
        sent_by(w2_s.at[far], wo.at[three, quarter])
        side = 1 - half if far else half
        ref = wo.at[pl.ds(pl.multiple_of(side * 4, 4), 4), quarter]
        for shift in (1, 2, 3):
            send(ref, ref, w3_s.at[far], w3_r.at[far], (row, y_col(shift)))
        sent_by(w3_s.at[far], wo.at[pl.ds(0, 4), pl.ds(0, 48)])

    for k in range(CHUNKS):
        if k == 1:
            weights_y(0)
        if k == 2:
            weights_x()
        if k == 3:
            weights_y(1)
        if k < 2:
            window_block(k, k + 1)
        else:
            outer_edge(third if k == 2 else fourth, k == 3)
            window_block(k, third if k == 2 else fourth)
        own[part(k), :] = norm(merged[part(k), :].astype(F32), coarse_scales)
        for t, target in enumerate((row, far_row)):
            send(
                own.at[part(k)],
                tok.at[half, xx >> 1, xx & 1, part(k)],
                z_s.at[t],
                z_r.at[k],
                (target, far_col),
            )
    for t in range(2):
        sent_by(z_s.at[t], own)

    def blocks(shift, k):
        at = (xx + shift) & 3
        return tok.at[:, at >> 1, at & 1, part(k)]

    def one(side, shift, k):
        at = (xx + shift) & 3
        return tok.at[side, at >> 1, at & 1, part(k)]

    def gather(k):
        ref = blocks(0, k)
        arrive(ref, z_r.at[k], z_s.at[0])
        send(ref, ref, xr_s.at[0], xr_r.at[k], (x_row(1), col))
        send(ref, ref, xl_s.at[0], xl_r.at[k], (x_row(3), col))

    def relay(k):
        arrive(blocks(3, k), xr_r.at[k], xr_s.at[0])
        ref = one(0, 3, k)
        send(ref, ref, xf_s.at[0], xf_r.at[k], (x_row(1), col))
        arrive(blocks(1, k), xl_r.at[k], xl_s.at[0])
        ref = one(1, 1, k)
        send(ref, ref, xf_s.at[1], xf_r.at[k], (x_row(3), col))

    def finish(k):
        arrive(blocks(2, k), xf_r.at[k], xf_s.at[0])

    left = iota((8 * PER, 128), 1) < 64

    def keep_proj(result, which, k):
        both, value = result[:, 0:128], result[:, 128:256]
        for ref, array in (
            (asked_all, jnp.where(left, both, 0.0)),
            (keys_all, pltpu.roll(both, 64, 1)),
            (values_all, jnp.where(left, value, 1.0)),
        ):
            ref[:, :, which, k * PER : (k + 1) * PER, :] = array.astype(BF).reshape(2, 4, PER, 128)

    def project(k):
        tokens = tok[:, :, :, k * PER : (k + 1) * PER, :].reshape(8 * PER, WIDE)
        result = nt(tokens, w3[...])
        proj_s[k] = result[:, 256:512].astype(BF)
        send(proj_s.at[k], proj_r.at[k], sib_s.at[0], sib_r.at[k], (sibling, col))
        keep_proj(result[:, 0:256], core, k)

    def from_sibling(k):
        arrive(proj_r.at[k], sib_r.at[k], sib_s.at[0])
        keep_proj(proj_r[k].astype(F32), 1 - core, k)

    arrive(wt_other, wt_r.at[0], wt_s.at[0])
    w3[256:320, :] = (wt_other[0:64, :].astype(F32) * 0.125).astype(BF)
    w3[320:448, :] = wt_other[64:192, :]
    w3[448:512, :] = jnp.zeros((64, WIDE), BF)

    gather(0)
    relay(0)
    for k in range(1, CHUNKS):
        gather(k)
        finish(k - 1)
        relay(k)
        project(k - 1)
        if k > 1:
            from_sibling(k - 2)
    finish(CHUNKS - 1)
    project(CHUNKS - 1)
    from_sibling(CHUNKS - 2)
    from_sibling(CHUNKS - 1)

    low = iota((32, 128), 1) < 64
    keys = keys_all[...].reshape(WIDE, 128)
    values = values_all[...].reshape(WIDE, 128)

    turns = (2, 1, 3, 0)

    def score(turn):
        return nt(asked_all[:, ((xx + turns[turn]) & 3)].reshape(256, 128), keys)

    for sem in (xr_s.at[0], xl_s.at[0]):
        sent_by(sem, tok.at[:, 0, 0])
    for side in range(2):
        sent_by(xf_s.at[side], tok.at[side, 0, 0])
    sent_by(sib_s.at[0], proj_s)

    scores = score(0)
    for turn in range(4):
        following = score(turn + 1) if turn < 3 else None
        weights = jnp.exp(scores - jnp.max(scores, 1, keepdims=True)).astype(BF)
        mixed = mm(weights, values)
        mixed = mixed / pltpu.roll(mixed, 64, 1)
        for which in range(4):
            at = 64 * which
            packed = jnp.where(low, mixed[at : at + 32], pltpu.roll(mixed[at + 32 : at + 64], 64, 1))
            ret_s[turn, which // 2, which % 2] = packed.astype(BF)
        for side in range(2):
            target = side * 8 + ((xx + turns[turn]) & 3) * 2 + core
            send(ret_s.at[turn, side], ret_r.at[turn, half], back_s.at[0], back_r.at[turn], (target, far_col))
        scores = following

    load_up.wait()
    load_skip.wait()
    load_solver.wait()
    pixels = merged[...].astype(F32)
    table = solver_ref[...]
    table = jnp.where(iota(table.shape, 1) == step_ref[0], table, 0.0)
    keep = jnp.sum(table[0:1], 1, keepdims=True)
    gain = jnp.sum(table[1:2], 1, keepdims=True)
    skip = skip_ref[...].reshape(1, 256)
    base = keep * noisy_m[...].astype(F32) + gain * (jnp.concatenate([skip] * 4, 1) * pixels)
    i = iota((256, 256), 0)
    r, c = i >> 3, i & 7
    block = r >> 3
    spot = jnp.where((block == 1) | (block == 2), block - 1, jnp.where(block == third, 2, 3))
    source = (2 * (r & 1) + (c & 1)) * 64 + spot * 16 + ((r >> 1) & 3) * 4 + (c >> 1)
    unshuffle = (iota((256, 256), 1) == source).astype(F32).astype(BF)
    for far in range(2):
        arrive(wo.at[pl.ds(0, 4), pl.ds(0, 48)], w3_r.at[far], w3_s.at[far])
    for d in range(8):

        @pl.when(there[d])
        def _():
            halo_copy(d).wait_send()

    for piece in range(3):

        @pl.when(seam[piece])
        def _():
            seam_copy(piece).wait_send()

        @pl.when(handed[piece])
        def _():
            hand_copy(piece).wait_send()

    wait_sent()

    def head_rows(turn, which):
        even, odd = ret_r[turn, 0, which].astype(F32), ret_r[turn, 1, which].astype(F32)
        first = jnp.where(low, even, pltpu.roll(odd, 64, 1))
        second = jnp.where(low, pltpu.roll(even, 64, 1), odd)
        return jnp.concatenate([first, second], 0).astype(BF)

    shares = [None, None]
    for couple in range(2):
        weight = []
        for turn in (2 * couple, 2 * couple + 1):
            arrive(ret_r.at[turn], back_r.at[turn], back_s.at[0])
            from_x = (xx + 4 - turns[turn]) & 3
            weight += [wo[from_x], wo[4 + from_x]]
        weight = jnp.concatenate(weight, 0)
        for at, which in enumerate((1 - core, core)):
            heads = jnp.concatenate([head_rows(2 * couple, which), head_rows(2 * couple + 1, which)], 1)
            share = mm(heads, weight)
            shares[at] = share if couple == 0 else shares[at] + share
            if couple == 1 and at == 0:
                share_s[...] = shares[0].astype(BF)
                send(share_s, share_r, share_sems.at[0], share_sems.at[1], (sibling, col))
    coarse_next = pixels + shares[1]
    arrive(share_r, share_sems.at[1], share_sems.at[0])
    coarse_next = coarse_next + share_r[...].astype(F32)
    upsampled = mm(coarse_next.astype(BF), wup[...])
    sent_by(back_s.at[0], ret_s)
    sent_by(share_sems.at[0], share_s)
    wait_sent()
    result = base + gain * upsampled
    stacked = jnp.concatenate([result[:, ab * 256 : ab * 256 + 256] for ab in range(4)], 0)
    upper = stacked.astype(BF)
    lower = (stacked - upper.astype(F32)).astype(BF)
    out_ref[...] = (mm(unshuffle, upper) + mm(unshuffle, lower)).reshape(32, 8, 256)


def shards(
    noisy_image,
    time_index,
    solver_index,
    time_gains,
    pixel_qkv,
    pixel_out,
    coarse_gains,
    coarse_qkv,
    coarse_out,
    upsample_weight,
    skip_gain,
    solver_table,
):
    vmem = pl.BlockSpec(memory_space=pltpu.VMEM)
    smem = pl.BlockSpec(memory_space=pltpu.SMEM)
    hbm = pl.BlockSpec(memory_space=pltpu.HBM)
    dma = pltpu.SemaphoreType.DMA
    return pl.pallas_call(
        kernel,
        out_shape=jax.ShapeDtypeStruct((32, 8, 256), F32),
        in_specs=[smem] * 2 + [hbm] * 10,
        out_specs=vmem,
        scratch_shapes=[
            pltpu.VMEM((32, 8, 256), BF),
            pltpu.VMEM((2, 32), F32),
            pltpu.VMEM((32, 256), F32),
            pltpu.VMEM((256, 768), BF),
            pltpu.VMEM((256, 256), BF),
            pltpu.VMEM((32, WIDE), F32),
            pltpu.VMEM((256,), F32),
            pltpu.VMEM((320, 256), BF),
            pltpu.VMEM((160, 256), BF),
            pltpu.VMEM((160, 256), BF),
            pltpu.VMEM((128, 256), BF),
            pltpu.VMEM((128, 256), BF),
            pltpu.VMEM((64, 256), BF),
            pltpu.VMEM((320, 512), BF),
            pltpu.VMEM((320, 512), BF),
            pltpu.VMEM((256, 256), BF),
            pltpu.VMEM((64, WIDE), BF),
            pltpu.VMEM((64, WIDE), BF),
            pltpu.VMEM((64, WIDE), BF),
            pltpu.VMEM((2, 2, 2, 64, WIDE), BF),
            pltpu.VMEM((192, WIDE), BF),
            pltpu.VMEM((192, WIDE), BF),
            pltpu.VMEM((512, WIDE), BF),
            pltpu.VMEM((8, 64, WIDE), BF),
            pltpu.VMEM((WIDE, WIDE), BF),
            pltpu.VMEM((2, 4, 2, 64, 128), BF),
            pltpu.VMEM((2, 4, 2, 64, 128), BF),
            pltpu.VMEM((2, 4, 2, 64, 128), BF),
            pltpu.VMEM((CHUNKS, 8 * PER, 256), BF),
            pltpu.VMEM((CHUNKS, 8 * PER, 256), BF),
            pltpu.VMEM((4, 2, 2, 32, 128), BF),
            pltpu.VMEM((4, 2, 2, 32, 128), BF),
            pltpu.VMEM((64, WIDE), BF),
            pltpu.VMEM((64, WIDE), BF),
            dma((8,)),
            dma((8,)),
            dma((3,)),
            dma((3,)),
            dma((3,)),
            dma((2,)),
            dma((CHUNKS,)),
            dma((1,)),
            dma((CHUNKS,)),
            dma((1,)),
            dma((CHUNKS,)),
            dma((2,)),
            dma((CHUNKS,)),
            dma((1,)),
            dma((CHUNKS,)),
            dma((1,)),
            dma((1,)),
            dma((2,)),
            dma((2,)),
            dma((2,)),
            dma((2,)),
            dma((1,)),
            dma((1,)),
            dma((2,)),
            dma((1,)),
            dma((4,)),
            dma((10,)),
        ],
        compiler_params=pltpu.CompilerParams(
            collective_id=0, has_side_effects=True, vmem_limit_bytes=48 * 1024 * 1024
        ),
        cost_estimate=pl.CostEstimate(flops=2_000_000_000, bytes_accessed=8_000_000, transcendentals=1_300_000),
    )(
        time_index,
        solver_index,
        *(
            pltpu.with_memory_space_constraint(array, pltpu.HBM)
            for array in (
                noisy_image,
                solver_table.T,
                time_gains,
                pixel_qkv,
                pixel_out,
                coarse_gains,
                skip_gain,
                coarse_qkv.reshape(coarse_qkv.shape[0], coarse_qkv.shape[2]).T,
                coarse_out,
                upsample_weight,
            )
        ),
    )


def solution(mesh):
    placed = (
        P("row", "col", None),
        P(),
        P(),
        P(),
        P(),
        P(),
        P(),
        P(None, "row", None),
        P("row", None),
        P(),
        P(),
        P(),
    )
    return jax.shard_map(
        shards, mesh=mesh, in_specs=placed, out_specs=P("row", "col", None), check_vma=False
    )
```
